512 devices in a mesh: blk: 32 (over x, z_lo), col: 16 (over z_hi, y, core).
Axes of the slice: x: 4, y: 4, z: 16 (z_hi: 2, z_lo: 8; z = z_hi * 8 + z_lo), core: 2. Of those that a mesh axis runs over, the one named last changes fastest.
Arguments:
- probes: bfloat16 [8, 8, 32, 512], P(None, None, 'blk'), may hold values from -6 to 6
- diag_tiles: bfloat16 [8, 32, 512, 512], P(None, 'blk', 'col'), may hold values from -0.25 to 0.25
- left_factors: bfloat16 [8, 32, 2, 32, 32, 512], P(None, 'blk', None, 'col'), may hold values from -0.09375 to 0.09375
- right_factors: bfloat16 [8, 32, 2, 32, 32, 512], P(None, 'blk', None, 'col'), may hold values from -0.25 to 0.25
- ranks: int32 [8, 32, 2, 32], P(None, 'blk', None, 'col'), may hold values from 8 to 32
- present: int32 [8, 32, 2, 32], P(None, 'blk', None, 'col'), may hold values from 0 to 1, as said below
Outputs:
- product: float32 [8, 8, 32, 512], P(None, None, 'blk')
The draws below stay inside these ranges and needn't reach their ends.
Inputs may be any that keep to these rules, and one draw needn't show every extreme that they name: A tile (i, i - d) is present exactly when i - d >= 0 and d is at most the band length of block row i; band lengths lie between 16 and 64, and some row's is 64.
All inputs are finite; a program needn't handle non-finite values.
Results may differ from the reference program's by a relative error of at most 0.0016.
Values may be sent and summed in bfloat16 or wider, within the bound.
A program may use at most 64 MiB of HBM per device.

```python
import jax
import jax.numpy as jnp

B = 512
K = 32
P_SIZE = 8
Q = 2
R = 8
CYCLE = 32
NB = 256
W = 64
N_BLK = 32


def draw_present(key, part):
    key = jax.random.fold_in(key, 11)
    first_key, second_key = jax.random.split(key)
    band = jax.random.randint(first_key, (NB,), W // 4, W + 1)
    chosen = jax.random.randint(second_key, (), 0, NB)
    row_ids = jnp.arange(NB)
    band = jnp.where(row_ids == chosen, W, band)
    offsets = jnp.arange(W) + 1
    stored = (offsets[None, :] <= band[:, None]) & (row_ids[:, None] - offsets[None, :] >= 0)
    return stored.astype(jnp.int32).reshape(R, CYCLE, Q, CYCLE)


def with_ends(values, own_key, smallest, largest):
    longest = values.shape.index(max(values.shape))
    spots = []
    for shift in (0, 1):
        where = [jax.random.randint(jax.random.fold_in(own_key, axis), (), 0, length) for axis, length in enumerate(values.shape)]
        where[longest] = (where[longest] + shift) % values.shape[longest]
        spots.append(tuple(where))
    return values.at[spots[0]].set(smallest).at[spots[1]].set(largest)


def steps_of(key, dims, cuts, least, top_value):
    loudness, own = 1.0, jax.random.fold_in(key, 6)
    for position, blocks in cuts:
        draws = jnp.exp(jax.random.uniform(jax.random.fold_in(own, position), (blocks,), jnp.float32, least / len(cuts), top_value / len(cuts)))
        loudness = loudness * jnp.repeat(draws, dims[position] // blocks).reshape([-1 if axis == position else 1 for axis in range(len(dims))])
    return loudness


def bell_draw(own_key, dims, scale, reach, shards=(), dtype=jnp.bfloat16):
    entries = scale * jax.random.normal(own_key, dims, jnp.float32)
    if shards:
        entries = entries * steps_of(own_key, dims, shards, -0.22, 0.18)
    return jnp.clip(entries, -reach, reach).astype(dtype)


def setup_inputs(seed: int = 0) -> dict:
    streams_of = jax.random.split(jax.random.key(seed), 7)
    probes = bell_draw(streams_of[0], (P_SIZE, R, CYCLE, B), 1.0, 6.0, ((2, 32),))
    diag_tiles = bell_draw(streams_of[1], (R, CYCLE, B, B), B ** -0.5, 0.25, ((1, 32), (2, 16)))
    left_factors = bell_draw(streams_of[2], (R, CYCLE, Q, CYCLE, K, B), (2 * K * W) ** -0.5, 0.09375, ((1, 32), (3, 16)))
    right_factors = bell_draw(streams_of[3], (R, CYCLE, Q, CYCLE, K, B), B ** -0.5, 0.25, ((1, 32), (3, 16)))
    ranks = with_ends(jax.random.randint(streams_of[4], (R, CYCLE, Q, CYCLE), K // 4, K + 1), jax.random.fold_in(streams_of[4], 1), K // 4, K).astype(jnp.int32)
    present = draw_present(jax.random.fold_in(streams_of[6], 71), 0)
    return dict(probes=probes, diag_tiles=diag_tiles, left_factors=left_factors, right_factors=right_factors, ranks=ranks, present=present)


def reference(probes, diag_tiles, left_factors, right_factors, ranks, present):
    block_rows = R * N_BLK
    band_width = Q * N_BLK
    probe_rows = jnp.transpose(probes.reshape(P_SIZE, block_rows, B), (1, 0, 2)).astype(jnp.float32)
    left_all = left_factors.reshape(block_rows, band_width, K, B)
    right_all = right_factors.reshape(block_rows, band_width, K, B)
    rank_all = ranks.reshape(block_rows, band_width)
    kept_all = present.reshape(block_rows, band_width)
    keep = ((jnp.arange(K)[None, None, :] < rank_all[:, :, None]) & (kept_all[:, :, None] == 1)).astype(jnp.float32)
    dense = diag_tiles.reshape(block_rows, B, B).astype(jnp.float32)
    combined = jnp.einsum('iab,ipb->ipa', dense, probe_rows)
    for offset in range(band_width):
        distance = offset + 1
        if distance < block_rows:
            earlier = jnp.concatenate([jnp.zeros((distance, P_SIZE, B), jnp.float32), probe_rows[:block_rows - distance]], 0)
        else:
            earlier = jnp.zeros((block_rows, P_SIZE, B), jnp.float32)
        left_tile = left_all[:, offset].astype(jnp.float32)
        right_tile = right_all[:, offset].astype(jnp.float32)
        keep_here = keep[:, offset, :, None]
        coeffs = (jnp.einsum('ikb,ipb->ikp', right_tile, earlier) * keep_here).astype(jnp.bfloat16)
        combined = combined + jnp.einsum('ikp,ikb->ipb', coeffs.astype(jnp.float32), left_tile)
        reverse_coef = (jnp.einsum('ikb,ipb->ikp', left_tile, probe_rows) * keep_here).astype(jnp.bfloat16)
        image_rows = jnp.einsum('ikp,ikb->ipb', reverse_coef.astype(jnp.float32), right_tile)
        if distance < block_rows:
            moved_rows = jnp.concatenate([image_rows[distance:], jnp.zeros((distance, P_SIZE, B), jnp.float32)], 0)
            combined = combined + moved_rows
    return jnp.transpose(combined, (1, 0, 2)).reshape(P_SIZE, R, N_BLK, B)
```

```python
import functools

import jax
import jax.numpy as jnp
from jax import lax
from jax.experimental import pallas as pl
from jax.experimental.pallas import tpu as pltpu
from jax.sharding import PartitionSpec as P

MESH = pl.DeviceIdType.MESH
BF16 = jnp.bfloat16
F32 = jnp.float32

NBLK = 32
HALF = 8
ZRING = 16
ZLOW = 8


def dot(a, b):
    return lax.dot_general(a, b, (((1,), (0,)), ((), ())), preferred_element_type=F32)


def dot_t(a, b):
    return lax.dot_general(a, b, (((1,), (1,)), ((), ())), preferred_element_type=F32)


def partners(b, c, s):
    zl = lax.rem(b, ZLOW)
    zh = lax.div(c, HALF)
    g = lax.rem(c, HALF)
    z = zh * ZLOW + zl
    flip = g if s == 0 else g + 1 - 2 * lax.rem(g, 2)
    src_b = lax.rem(b + 2 * NBLK - (2 * c + 1 + s), NBLK)
    src_h = lax.rem(lax.div(z - lax.rem(src_b, ZLOW) + ZRING + 4, ZLOW), 2)
    shift = 2 * flip + 1 + s
    dst_h = lax.rem(lax.div(lax.rem(zl + shift, ZLOW) - z + ZRING + 4, ZLOW), 2)
    dst_b = lax.rem(b + shift + 16 * dst_h, NBLK)
    return (src_b, src_h * HALF + flip), (dst_b, dst_h * HALF + flip)


def quarter(b, c, up):
    zl = lax.rem(b, ZLOW)
    z = lax.rem(lax.div(c, HALF) * ZLOW + zl + up, ZRING)
    return b - zl + lax.rem(z, ZLOW), lax.div(z, ZLOW) * HALF + lax.rem(c, HALF)


def kernel(
    x_hbm, d_hbm, u_hbm, v_hbm, rank_hbm, pres_hbm, out,
    x_v, d_v, u_v, v_v, rank_v, pres_v, y_v, car_out, car_in, rs_out, rs_in, zx_out, zx_in,
    in_sem, y_ssem, y_rsem, car_ssem, car_rsem, rs_ssem, rs_rsem, zx_ssem, zx_rsem, ag_ssem, ag_rsem, met_sem,
):
    def load(i, src, dst):
        copy = pltpu.make_async_copy(src, dst, in_sem.at[i])
        copy.start()
        return copy

    small = [load(0, rank_hbm, rank_v), load(1, pres_hbm, pres_v)]
    x_load = load(2, x_hbm, x_v)
    tiles = [
        [load(3 + 2 * s, u_hbm.at[:, :, s], u_v.at[:, :, s]), load(4 + 2 * s, v_hbm.at[:, :, s], v_v.at[:, :, s])]
        for s in range(2)
    ]
    d_load = load(7, d_hbm, d_v)

    b = lax.axis_index("blk")
    c = lax.axis_index("col")
    pairs = [partners(b, c, s) for s in range(2)]
    g = lax.rem(c, HALF)
    base = c - g
    far_first = (4, 5, 3, 2, 6, 7, 1)
    ids = [lax.rem(g + o, HALF) for o in far_first]
    group = [(b, base + i) for i in ids]
    across = (b, lax.rem(c + HALF, 2 * HALF))
    above, below = quarter(b, c, 4), quarter(b, c, 12)

    barrier = pltpu.get_barrier_semaphore()
    peers = [pairs[0][0], pairs[1][0], pairs[0][1], pairs[1][1], above, below] + group
    for peer in peers:
        pl.semaphore_signal(barrier, inc=1, device_id=peer, device_id_type=MESH)

    def remote(src, dst, ssem, rsem, device):
        return pltpu.make_async_remote_copy(
            src_ref=src, dst_ref=dst, send_sem=ssem, recv_sem=rsem, device_id=device, device_id_type=MESH
        )

    def wait_bytes(ref, sem):
        pltpu.make_async_copy(ref, ref, sem).wait()

    y_copies = [remote(x_hbm, y_v.at[s], y_ssem.at[s], y_rsem.at[s], pairs[s][1]) for s in range(2)]
    pl.semaphore_wait(barrier, len(peers))
    for copy in y_copies:
        copy.start()
    pl.semaphore_signal(met_sem, inc=1, device_id=below, device_id_type=MESH)

    for copy in small:
        copy.wait()
    lane = lax.broadcasted_iota(jnp.int32, (8, 512), 1)
    row = lax.broadcasted_iota(jnp.int32, (8, 512), 0)
    lane_r = lane >> 6
    lane_q = (lane >> 5) & 1
    lane_k = (lane & 31).astype(F32)
    spread = (row == lane_r).astype(BF16)
    height = [dot((rank_v[q] * pres_v[q]).astype(F32).astype(BF16), spread) for q in range(2)]
    kept, shift = [], []
    for s in range(2):
        kept.append(lane_k < jnp.where(lane_q == 0, height[0][s : s + 1], height[1][s : s + 1]))
        shift.append(lane_q + jnp.where(b < 2 * c + 1 + s, 1, 0))

    def pick(a, step, s, rows):
        a = a.reshape(8, 8, 512)
        once, twice = pltpu.roll(a, step % 8, 1), pltpu.roll(a, 2 * step % 8, 1)
        a = jnp.where(shift[s][None] == 0, a, jnp.where(shift[s][None] == 1, once, twice))
        return jnp.where((kept[s] & (lane_r == rows))[None], a, 0.0).reshape(64, 512).astype(BF16)

    def section(ref, s):
        return ref[:, :, s].reshape(512, 512)

    x_load.wait()
    x = x_v[...]
    car_copies = []
    for s in range(2):
        tiles[s][0].wait()
        t = pick(dot_t(x, section(u_v, s)), -1, s, row + shift[s])
        tiles[s][1].wait()
        car_out[s] = dot(t, section(v_v, s)).astype(BF16)
        copy = remote(car_out.at[s], car_in.at[s], car_ssem.at[s], car_rsem.at[s], pairs[s][0])
        copy.start()
        car_copies.append(copy)

    d_load.wait()
    dg = dot_t(x, d_v[...]).reshape(8, 8, 256)
    dg = jnp.where((lane[:, :256] >> 5 == row[:, :256])[None], dg, 0.0).reshape(64, 256)
    dg = dg[:, :128] + dg[:, 128:]
    dg = dg + pltpu.roll(dg, 64, 1)
    dg = dg + pltpu.roll(dg, 32, 1)
    total = jnp.concatenate([dg] * 4, 1).reshape(8, 8, 512)
    total = jnp.where((lane >> 5 == c)[None], total, 0.0).reshape(64, 512)

    for s in range(2):
        y_copies[s].wait_recv()
        a = pick(dot_t(y_v[s], section(v_v, s)), 1, s, row)
        total = total + dot(a, section(u_v, s))
    for s in range(2):
        car_copies[s].wait_recv()
        total = total + car_in[s].astype(F32)

    rs_out[...] = total.reshape(8, 8, 512)
    for i, peer in zip(ids, group):
        remote(rs_out.at[i], rs_in.at[g], rs_ssem, rs_rsem, peer).start()
    rs_in[g] = rs_out[g]
    for copy in y_copies + car_copies:
        copy.wait_send()
    wait_bytes(rs_in.at[pl.ds(0, HALF - 1)], rs_rsem)
    part = rs_in[0]
    for p in range(1, HALF):
        part = part + rs_in[p]

    zx_out[...] = part
    zx_copy = remote(zx_out, zx_in, zx_ssem, zx_rsem, across)
    pl.semaphore_wait(met_sem, 1)
    zx_copy.start()
    wait_bytes(rs_out.at[pl.ds(0, HALF - 1)], rs_ssem)
    zx_copy.wait_recv()
    whole = part + zx_in[...]
    for k in range(4):
        out[pl.ds(32 * g + k, 8, stride=4), :] = whole[:, 128 * k : 128 * k + 128]

    mine = out.at[pl.ds(pl.multiple_of(32 * g, 32), 32)]
    for peer in group:
        remote(mine, mine, ag_ssem, ag_rsem, peer).start()
    zx_copy.wait_send()
    others = out.at[pl.ds(0, 32 * (HALF - 1))]
    wait_bytes(others, ag_rsem)
    wait_bytes(others, ag_ssem)


def shards(probes, diag_tiles, left_factors, right_factors, ranks, present):
    hbm = pl.BlockSpec(memory_space=pltpu.HBM)
    dma = pltpu.SemaphoreType.DMA
    out = pl.pallas_call(
        kernel,
        out_shape=pltpu.VMEM((256, 128), F32),
        in_specs=[hbm] * 6,
        out_specs=pl.BlockSpec(memory_space=pltpu.VMEM),
        scratch_shapes=[
            pltpu.VMEM((64, 512), BF16),
            pltpu.VMEM((256, 512), BF16),
            pltpu.VMEM((8, 2, 2, 32, 512), BF16),
            pltpu.VMEM((8, 2, 2, 32, 512), BF16),
            pltpu.VMEM((2, 2, 8), jnp.int32),
            pltpu.VMEM((2, 2, 8), jnp.int32),
            pltpu.VMEM((2, 64, 512), BF16),
            pltpu.VMEM((2, 64, 512), BF16),
            pltpu.VMEM((2, 64, 512), BF16),
            pltpu.VMEM((8, 8, 512), F32),
            pltpu.VMEM((8, 8, 512), F32),
            pltpu.VMEM((8, 512), F32),
            pltpu.VMEM((8, 512), F32),
            dma((8,)),
            dma((2,)),
            dma((2,)),
            dma((2,)),
            dma((2,)),
            dma,
            dma,
            dma,
            dma,
            dma,
            dma,
            pltpu.SemaphoreType.REGULAR,
        ],
        compiler_params=pltpu.CompilerParams(
            collective_id=0, has_side_effects=True, vmem_limit_bytes=60 * 1024 * 1024
        ),
        cost_estimate=pl.CostEstimate(flops=300_000_000, bytes_accessed=2_500_000, transcendentals=0),
    )(
        probes.reshape(64, 512),
        diag_tiles.reshape(256, 512),
        left_factors[:, 0],
        right_factors[:, 0],
        jnp.transpose(ranks[:, 0], (1, 2, 0)),
        jnp.transpose(present[:, 0], (1, 2, 0)),
    )
    return out.reshape(8, 8, 1, 512)


def solution(mesh):
    return jax.shard_map(
        shards,
        mesh=mesh,
        in_specs=(
            P(None, None, "blk", None),
            P(None, "blk", "col", None),
            P(None, "blk", None, "col", None, None),
            P(None, "blk", None, "col", None, None),
            P(None, "blk", None, "col"),
            P(None, "blk", None, "col"),
        ),
        out_specs=P(None, None, "blk", None),
        check_vma=False,
    )
```

```python
import functools

import jax
import jax.numpy as jnp
from jax import lax
from jax.experimental import pallas as pl
from jax.experimental.pallas import tpu as pltpu
from jax.sharding import PartitionSpec as P

MESH = pl.DeviceIdType.MESH
BF16 = jnp.bfloat16
F32 = jnp.float32

NBLK = 32
HALF = 8
ZRING = 16
ZLOW = 8


def dot(a, b):
    return lax.dot_general(a, b, (((1,), (0,)), ((), ())), preferred_element_type=F32)


def dot_t(a, b):
    return lax.dot_general(a, b, (((1,), (1,)), ((), ())), preferred_element_type=F32)


def partners(b, c, s):
    zl = lax.rem(b, ZLOW)
    zh = lax.div(c, HALF)
    g = lax.rem(c, HALF)
    z = zh * ZLOW + zl
    flip = g if s == 0 else g + 1 - 2 * lax.rem(g, 2)
    src_b = lax.rem(b + 2 * NBLK - (2 * c + 1 + s), NBLK)
    src_h = lax.rem(lax.div(z - lax.rem(src_b, ZLOW) + ZRING + 4, ZLOW), 2)
    shift = 2 * flip + 1 + s
    dst_h = lax.rem(lax.div(lax.rem(zl + shift, ZLOW) - z + ZRING + 4, ZLOW), 2)
    dst_b = lax.rem(b + shift + 16 * dst_h, NBLK)
    return (src_b, src_h * HALF + flip), (dst_b, dst_h * HALF + flip)


def quarter(b, c, up):
    zl = lax.rem(b, ZLOW)
    z = lax.rem(lax.div(c, HALF) * ZLOW + zl + up, ZRING)
    return b - zl + lax.rem(z, ZLOW), lax.div(z, ZLOW) * HALF + lax.rem(c, HALF)


def kernel(
    x_hbm, d_hbm, u_hbm, v_hbm, rank_hbm, pres_hbm, out,
    x_v, d_v, u_v, v_v, rank_v, pres_v, y_v, car_out, car_in, rs_out, rs_in, zx_out, zx_in,
    in_sem, y_ssem, y_rsem, car_ssem, car_rsem, rs_ssem, rs_rsem, zx_ssem, zx_rsem, ag_ssem, ag_rsem, met_sem,
):
    b = lax.axis_index("blk")
    c = lax.axis_index("col")
    barrier = pltpu.get_barrier_semaphore()

    def greet(peers):
        for peer in peers:
            pl.semaphore_signal(barrier, inc=1, device_id=peer, device_id_type=MESH)

    def load(i, src, dst):
        copy = pltpu.make_async_copy(src, dst, in_sem.at[i])
        copy.start()
        return copy

    pairs = [partners(b, c, s) for s in range(2)]
    greet([pairs[0][0], pairs[1][0], pairs[0][1], pairs[1][1]])
    small = [load(0, rank_hbm, rank_v), load(1, pres_hbm, pres_v)]
    x_load = load(2, x_hbm, x_v)
    above, below = quarter(b, c, 4), quarter(b, c, 12)
    g = lax.rem(c, HALF)
    base = c - g
    far_first = (4, 5, 3, 2, 6, 7, 1)
    ids = [lax.rem(g + o, HALF) for o in far_first]
    group = [(b, base + i) for i in ids]
    greet([above, below] + group)
    tiles = [
        [load(3 + 2 * s, u_hbm.at[:, :, s], u_v.at[:, :, s]), load(4 + 2 * s, v_hbm.at[:, :, s], v_v.at[:, :, s])]
        for s in range(2)
    ]
    d_load = load(7, d_hbm, d_v)
    across = (b, lax.rem(c + HALF, 2 * HALF))

    def remote(src, dst, ssem, rsem, device):
        return pltpu.make_async_remote_copy(
            src_ref=src, dst_ref=dst, send_sem=ssem, recv_sem=rsem, device_id=device, device_id_type=MESH
        )

    def wait_bytes(ref, sem):
        pltpu.make_async_copy(ref, ref, sem).wait()

    y_copies = [remote(x_v, y_v.at[s], y_ssem.at[s], y_rsem.at[s], pairs[s][1]) for s in range(2)]
    for copy in small:
        copy.wait()
    lane = lax.broadcasted_iota(jnp.int32, (8, 512), 1)
    row = lax.broadcasted_iota(jnp.int32, (8, 512), 0)
    lane_r = lane >> 6
    lane_q = (lane >> 5) & 1
    lane_k = (lane & 31).astype(F32)
    spread = (row == lane_r).astype(BF16)
    height = [dot((rank_v[q] * pres_v[q]).astype(F32).astype(BF16), spread) for q in range(2)]
    kept, shift = [], []
    for s in range(2):
        kept.append(lane_k < jnp.where(lane_q == 0, height[0][s : s + 1], height[1][s : s + 1]))
        shift.append(lane_q + jnp.where(b < 2 * c + 1 + s, 1, 0))

    def pick(a, step, s, rows):
        a = a.reshape(8, 8, 512)
        once, twice = pltpu.roll(a, step % 8, 1), pltpu.roll(a, 2 * step % 8, 1)
        a = jnp.where(shift[s][None] == 0, a, jnp.where(shift[s][None] == 1, once, twice))
        return jnp.where((kept[s] & (lane_r == rows))[None], a, 0.0).reshape(64, 512).astype(BF16)

    def section(ref, s):
        return ref[:, :, s].reshape(512, 512)

    x_load.wait()
    x = x_v[...]
    for s in range(2):
        tiles[s][0].wait()
        t = pick(dot_t(x, section(u_v, s)), -1, s, row + shift[s])
        tiles[s][1].wait()
        car_out[s] = dot(t, section(v_v, s)).astype(BF16)
    car_copies = [
        remote(car_out.at[s], car_in.at[s], car_ssem.at[s], car_rsem.at[s], pairs[s][0]) for s in range(2)
    ]

    pl.semaphore_wait(barrier, 6 + len(group))
    for copy in y_copies + car_copies:
        copy.start()
    pl.semaphore_signal(met_sem, inc=1, device_id=below, device_id_type=MESH)

    d_load.wait()
    dg = dot_t(x, d_v[...]).reshape(8, 8, 256)
    dg = jnp.where((lane[:, :256] >> 5 == row[:, :256])[None], dg, 0.0).reshape(64, 256)
    dg = dg[:, :128] + dg[:, 128:]
    dg = dg + pltpu.roll(dg, 64, 1)
    dg = dg + pltpu.roll(dg, 32, 1)
    total = jnp.concatenate([dg] * 4, 1).reshape(8, 8, 512)
    total = jnp.where((lane >> 5 == c)[None], total, 0.0).reshape(64, 512)

    for s in range(2):
        y_copies[s].wait_recv()
        a = pick(dot_t(y_v[s], section(v_v, s)), 1, s, row)
        total = total + dot(a, section(u_v, s))
    for s in range(2):
        car_copies[s].wait_recv()
        total = total + car_in[s].astype(F32)

    rs_out[...] = total.reshape(8, 8, 512)
    for i, peer in zip(ids, group):
        remote(rs_out.at[i], rs_in.at[g], rs_ssem, rs_rsem, peer).start()
    rs_in[g] = rs_out[g]
    for copy in y_copies + car_copies:
        copy.wait_send()
    wait_bytes(rs_in.at[pl.ds(0, HALF - 1)], rs_rsem)
    part = rs_in[0]
    for p in range(1, HALF):
        part = part + rs_in[p]

    zx_out[...] = part
    zx_copy = remote(zx_out, zx_in, zx_ssem, zx_rsem, across)
    pl.semaphore_wait(met_sem, 1)
    zx_copy.start()
    wait_bytes(rs_out.at[pl.ds(0, HALF - 1)], rs_ssem)
    zx_copy.wait_recv()
    whole = part + zx_in[...]
    for k in range(4):
        out[pl.ds(32 * g + k, 8, stride=4), :] = whole[:, 128 * k : 128 * k + 128]

    mine = out.at[pl.ds(pl.multiple_of(32 * g, 32), 32)]
    for peer in group:
        remote(mine, mine, ag_ssem, ag_rsem, peer).start()
    zx_copy.wait_send()
    others = out.at[pl.ds(0, 32 * (HALF - 1))]
    wait_bytes(others, ag_rsem)
    wait_bytes(others, ag_ssem)


def shards(probes, diag_tiles, left_factors, right_factors, ranks, present):
    hbm = pl.BlockSpec(memory_space=pltpu.HBM)
    dma = pltpu.SemaphoreType.DMA
    out = pl.pallas_call(
        kernel,
        out_shape=pltpu.VMEM((256, 128), F32),
        in_specs=[hbm] * 6,
        out_specs=pl.BlockSpec(memory_space=pltpu.VMEM),
        scratch_shapes=[
            pltpu.VMEM((64, 512), BF16),
            pltpu.VMEM((256, 512), BF16),
            pltpu.VMEM((8, 2, 2, 32, 512), BF16),
            pltpu.VMEM((8, 2, 2, 32, 512), BF16),
            pltpu.VMEM((2, 2, 8), jnp.int32),
            pltpu.VMEM((2, 2, 8), jnp.int32),
            pltpu.VMEM((2, 64, 512), BF16),
            pltpu.VMEM((2, 64, 512), BF16),
            pltpu.VMEM((2, 64, 512), BF16),
            pltpu.VMEM((8, 8, 512), F32),
            pltpu.VMEM((8, 8, 512), F32),
            pltpu.VMEM((8, 512), F32),
            pltpu.VMEM((8, 512), F32),
            dma((8,)),
            dma((2,)),
            dma((2,)),
            dma((2,)),
            dma((2,)),
            dma,
            dma,
            dma,
            dma,
            dma,
            dma,
            pltpu.SemaphoreType.REGULAR,
        ],
        compiler_params=pltpu.CompilerParams(
            collective_id=0, has_side_effects=True, vmem_limit_bytes=60 * 1024 * 1024
        ),
        cost_estimate=pl.CostEstimate(flops=300_000_000, bytes_accessed=2_500_000, transcendentals=0),
    )(
        probes.reshape(64, 512),
        diag_tiles.reshape(256, 512),
        left_factors[:, 0],
        right_factors[:, 0],
        jnp.transpose(ranks[:, 0], (1, 2, 0)),
        jnp.transpose(present[:, 0], (1, 2, 0)),
    )
    return out.reshape(8, 8, 1, 512)


def solution(mesh):
    return jax.shard_map(
        shards,
        mesh=mesh,
        in_specs=(
            P(None, None, "blk", None),
            P(None, "blk", "col", None),
            P(None, "blk", None, "col", None, None),
            P(None, "blk", None, "col", None, None),
            P(None, "blk", None, "col"),
            P(None, "blk", None, "col"),
        ),
        out_specs=P(None, None, "blk", None),
        check_vma=False,
    )
```

```python
import functools

import jax
import jax.numpy as jnp
from jax import lax
from jax.experimental import pallas as pl
from jax.experimental.pallas import tpu as pltpu
from jax.sharding import PartitionSpec as P

MESH = pl.DeviceIdType.MESH
BF16 = jnp.bfloat16
F32 = jnp.float32

NBLK = 32
HALF = 8
ZRING = 16
ZLOW = 8
CHUNK = 32


def dot(a, b):
    return lax.dot_general(a, b, (((1,), (0,)), ((), ())), preferred_element_type=F32)


def dot_t(a, b):
    return lax.dot_general(a, b, (((1,), (1,)), ((), ())), preferred_element_type=F32)


def partners(b, c, s):
    zl = lax.rem(b, ZLOW)
    zh = lax.div(c, HALF)
    g = lax.rem(c, HALF)
    z = zh * ZLOW + zl
    flip = g if s == 0 else g + 1 - 2 * lax.rem(g, 2)
    src_b = lax.rem(b + 2 * NBLK - (2 * c + 1 + s), NBLK)
    src_h = lax.rem(lax.div(z - lax.rem(src_b, ZLOW) + ZRING + 4, ZLOW), 2)
    shift = 2 * flip + 1 + s
    dst_h = lax.rem(lax.div(lax.rem(zl + shift, ZLOW) - z + ZRING + 4, ZLOW), 2)
    dst_b = lax.rem(b + shift + 16 * dst_h, NBLK)
    return (src_b, src_h * HALF + flip), (dst_b, dst_h * HALF + flip)


def quarter(b, c, up):
    zl = lax.rem(b, ZLOW)
    z = lax.rem(lax.div(c, HALF) * ZLOW + zl + up, ZRING)
    return b - zl + lax.rem(z, ZLOW), lax.div(z, ZLOW) * HALF + lax.rem(c, HALF)


def kernel(
    x_hbm, d_hbm, u_hbm, v_hbm, rank_hbm, pres_hbm, out,
    x_v, d_v, u_v, v_v, rank_v, pres_v, y_v, car_tmp, car_out, car_in, rs_out, rs_in, zx_out, zx_in,
    in_sem, y_ssem, y_rsem, car_ssem, car_rsem, rs_ssem, rs_rsem, zx_ssem, zx_rsem, ag_ssem, ag_rsem, met_sem, open_sem,
):
    b = lax.axis_index("blk")
    c = lax.axis_index("col")
    barrier = pltpu.get_barrier_semaphore()

    def greet(peers):
        for peer in peers:
            pl.semaphore_signal(barrier, inc=1, device_id=peer, device_id_type=MESH)

    def load(i, src, dst):
        copy = pltpu.make_async_copy(src, dst, in_sem.at[i])
        copy.start()
        return copy

    pairs = [partners(b, c, s) for s in range(2)]
    greet([pairs[0][0], pairs[1][0], pairs[0][1], pairs[1][1]])
    small = [load(0, rank_hbm, rank_v), load(1, pres_hbm, pres_v)]
    x_load = load(2, x_hbm, x_v)
    above, below = quarter(b, c, 4), quarter(b, c, 12)
    g = lax.rem(c, HALF)
    base = c - g
    far_first = (4, 5, 3, 2, 6, 7, 1)
    ids = [lax.rem(g + o, HALF) for o in far_first]
    group = [(b, base + i) for i in ids]
    greet([above, below] + group)
    tiles = [
        [load(3 + 2 * s, u_hbm.at[:, :, s], u_v.at[:, :, s]), load(4 + 2 * s, v_hbm.at[:, :, s], v_v.at[:, :, s])]
        for s in range(2)
    ]
    d_load = load(7, d_hbm, d_v)
    across = (b, lax.rem(c + HALF, 2 * HALF))

    def remote(src, dst, ssem, rsem, device):
        return pltpu.make_async_remote_copy(
            src_ref=src, dst_ref=dst, send_sem=ssem, recv_sem=rsem, device_id=device, device_id_type=MESH
        )

    def wait_bytes(ref, sem):
        pltpu.make_async_copy(ref, ref, sem).wait()

    y_copies = [remote(x_v, y_v.at[s], y_ssem.at[s], y_rsem.at[s], pairs[s][1]) for s in range(2)]
    for copy in small:
        copy.wait()
    lane = lax.broadcasted_iota(jnp.int32, (8, 512), 1)
    row = lax.broadcasted_iota(jnp.int32, (8, 512), 0)
    lane_r = lane >> 6
    lane_q = (lane >> 5) & 1
    lane_k = (lane & 31).astype(F32)
    spread = (row == lane_r).astype(BF16)
    height = [dot((rank_v[q] * pres_v[q]).astype(F32).astype(BF16), spread) for q in range(2)]
    kept, shift = [], []
    for s in range(2):
        kept.append(lane_k < jnp.where(lane_q == 0, height[0][s : s + 1], height[1][s : s + 1]))
        shift.append(lane_q + jnp.where(b < 2 * c + 1 + s, 1, 0))

    def pick(a, step, s, rows):
        a = a.reshape(8, 8, 512)
        once, twice = pltpu.roll(a, step % 8, 1), pltpu.roll(a, 2 * step % 8, 1)
        a = jnp.where(shift[s][None] == 0, a, jnp.where(shift[s][None] == 1, once, twice))
        return jnp.where((kept[s] & (lane_r == rows))[None], a, 0.0).reshape(64, 512).astype(BF16)

    def section(ref, s):
        return ref[:, :, s].reshape(512, 512)

    x_load.wait()
    x = x_v[...]
    for s in range(2):
        tiles[s][0].wait()
        t = pick(dot_t(x, section(u_v, s)), -1, s, row + shift[s])
        tiles[s][1].wait()
        image = dot(t, section(v_v, s))
        for k in range(4):
            car_tmp[s, pl.ds(k, 64, stride=4), :] = image[:, 128 * k : 128 * k + 128]
        car_out[s] = car_tmp[s].reshape(HALF, CHUNK, 128).astype(BF16)

    pl.semaphore_wait(barrier, 6 + len(group))
    for copy in y_copies:
        copy.start()
    for s in range(2):
        pl.semaphore_signal(open_sem.at[s], inc=1, device_id=pairs[s][1], device_id_type=MESH)
    pl.semaphore_signal(met_sem, inc=1, device_id=below, device_id_type=MESH)

    d_load.wait()
    dg = dot_t(x, d_v[...]).reshape(8, 8, 256)
    dg = jnp.where((lane[:, :256] >> 5 == row[:, :256])[None], dg, 0.0).reshape(64, 256)
    dg = dg[:, :128] + dg[:, 128:]
    dg = dg + pltpu.roll(dg, 64, 1)
    dg = dg + pltpu.roll(dg, 32, 1)
    total = jnp.concatenate([dg] * 4, 1).reshape(8, 8, 512)
    total = jnp.where((lane >> 5 == c)[None], total, 0.0).reshape(64, 512)

    at_home = c == 2 * HALF - 1
    for s in range(2):
        pl.semaphore_wait(open_sem.at[s], 1)
        src_b, src_c = pairs[s][0]
        src_base = src_c - lax.rem(src_c, HALF)
        for i in ids + [g]:
            src, dst = car_out.at[s, i], car_in.at[s, g]
            copy = remote(src, dst, car_ssem, car_rsem, (src_b, src_base + i))
            if s == 1 and i is g:
                inside = pltpu.make_async_copy(src, dst, car_rsem)
                pl.when(at_home)(lambda: inside.start())
                pl.when(jnp.logical_not(at_home))(lambda: copy.start())
            else:
                copy.start()

    for s in range(2):
        y_copies[s].wait_recv()
        a = pick(dot_t(y_v[s], section(v_v, s)), 1, s, row)
        total = total + dot(a, section(u_v, s))
    for k in range(4):
        rs_out[pl.ds(k, 64, stride=4), :] = total[:, 128 * k : 128 * k + 128]

    def chunk(i):
        return pl.ds(pl.multiple_of(CHUNK * i, CHUNK), CHUNK)

    for i, peer in zip(ids, group):
        remote(rs_out.at[chunk(i)], rs_in.at[g], rs_ssem, rs_rsem, peer).start()
    rs_in[g] = rs_out[chunk(g), :]
    for copy in y_copies:
        copy.wait_send()

    wait_bytes(car_in, car_rsem)
    part = car_in[0, 0].astype(F32)
    for j in range(1, 2 * HALF):
        part = part + car_in[j // HALF, j % HALF].astype(F32)
    wait_bytes(rs_in.at[pl.ds(0, HALF - 1)], rs_rsem)
    for j in range(HALF):
        part = part + rs_in[j]
    zx_out[...] = part
    zx_copy = remote(zx_out, zx_in, zx_ssem, zx_rsem, across)
    pl.semaphore_wait(met_sem, 1)
    zx_copy.start()
    wait_bytes(rs_in.at[pl.ds(0, HALF - 1)], rs_ssem)
    wait_bytes(car_out.at[0], car_ssem)
    pl.when(at_home)(lambda: wait_bytes(car_out.at[1, pl.ds(0, HALF - 1)], car_ssem))
    pl.when(jnp.logical_not(at_home))(lambda: wait_bytes(car_out.at[1], car_ssem))

    zx_copy.wait_recv()
    mine = out.at[chunk(g)]
    mine[...] = part + zx_in[...]
    for peer in group:
        remote(mine, mine, ag_ssem, ag_rsem, peer).start()
    zx_copy.wait_send()
    others = out.at[pl.ds(0, CHUNK * (HALF - 1))]
    wait_bytes(others, ag_rsem)
    wait_bytes(others, ag_ssem)


def shards(probes, diag_tiles, left_factors, right_factors, ranks, present):
    hbm = pl.BlockSpec(memory_space=pltpu.HBM)
    dma = pltpu.SemaphoreType.DMA
    out = pl.pallas_call(
        kernel,
        out_shape=pltpu.VMEM((256, 128), F32),
        in_specs=[hbm] * 6,
        out_specs=pl.BlockSpec(memory_space=pltpu.VMEM),
        scratch_shapes=[
            pltpu.VMEM((64, 512), BF16),
            pltpu.VMEM((256, 512), BF16),
            pltpu.VMEM((8, 2, 2, 32, 512), BF16),
            pltpu.VMEM((8, 2, 2, 32, 512), BF16),
            pltpu.VMEM((2, 2, 8), jnp.int32),
            pltpu.VMEM((2, 2, 8), jnp.int32),
            pltpu.VMEM((2, 64, 512), BF16),
            pltpu.VMEM((2, 256, 128), F32),
            pltpu.VMEM((2, HALF, CHUNK, 128), BF16),
            pltpu.VMEM((2, HALF, CHUNK, 128), BF16),
            pltpu.VMEM((256, 128), F32),
            pltpu.VMEM((HALF, CHUNK, 128), F32),
            pltpu.VMEM((CHUNK, 128), F32),
            pltpu.VMEM((CHUNK, 128), F32),
            dma((8,)),
            dma((2,)),
            dma((2,)),
            dma,
            dma,
            dma,
            dma,
            dma,
            dma,
            dma,
            dma,
            pltpu.SemaphoreType.REGULAR,
            pltpu.SemaphoreType.REGULAR((2,)),
        ],
        compiler_params=pltpu.CompilerParams(
            collective_id=0, has_side_effects=True, vmem_limit_bytes=60 * 1024 * 1024
        ),
        cost_estimate=pl.CostEstimate(flops=300_000_000, bytes_accessed=2_500_000, transcendentals=0),
    )(
        probes.reshape(64, 512),
        diag_tiles.reshape(256, 512),
        left_factors[:, 0],
        right_factors[:, 0],
        jnp.transpose(ranks[:, 0], (1, 2, 0)),
        jnp.transpose(present[:, 0], (1, 2, 0)),
    )
    return out.reshape(8, 8, 1, 512)


def solution(mesh):
    return jax.shard_map(
        shards,
        mesh=mesh,
        in_specs=(
            P(None, None, "blk", None),
            P(None, "blk", "col", None),
            P(None, "blk", None, "col", None, None),
            P(None, "blk", None, "col", None, None),
            P(None, "blk", None, "col"),
            P(None, "blk", None, "col"),
        ),
        out_specs=P(None, None, "blk", None),
        check_vma=False,
    )
```

```python
import functools

import jax
import jax.numpy as jnp
from jax import lax
from jax.experimental import pallas as pl
from jax.experimental.pallas import tpu as pltpu
from jax.sharding import PartitionSpec as P

MESH = pl.DeviceIdType.MESH
BF16 = jnp.bfloat16
F32 = jnp.float32

NBLK = 32
HALF = 8
ZRING = 16
ZLOW = 8
CHUNK = 32


def dot(a, b):
    return lax.dot_general(a, b, (((1,), (0,)), ((), ())), preferred_element_type=F32)


def dot_t(a, b):
    return lax.dot_general(a, b, (((1,), (1,)), ((), ())), preferred_element_type=F32)


def partners(b, c, s):
    zl = lax.rem(b, ZLOW)
    zh = lax.div(c, HALF)
    g = lax.rem(c, HALF)
    z = zh * ZLOW + zl
    flip = g + lax.rem(g, 2) * (HALF - 2 * g)
    src_b = lax.rem(b + 2 * NBLK - (2 * c + 1 + s), NBLK)
    src_h = lax.rem(lax.div(z - lax.rem(src_b, ZLOW) + ZRING + 4, ZLOW), 2)
    shift = 2 * flip + 1 + s
    dst_h = lax.rem(lax.div(lax.rem(zl + shift, ZLOW) - z + ZRING + 4, ZLOW), 2)
    dst_b = lax.rem(b + shift + 16 * dst_h, NBLK)
    return (src_b, src_h * HALF + flip), (dst_b, dst_h * HALF + flip)


def quarter(b, c, up):
    zl = lax.rem(b, ZLOW)
    z = lax.rem(lax.div(c, HALF) * ZLOW + zl + up, ZRING)
    return b - zl + lax.rem(z, ZLOW), lax.div(z, ZLOW) * HALF + lax.rem(c, HALF)


def kernel(
    x_hbm, d_hbm, u_hbm, v_hbm, rank_hbm, pres_hbm, out,
    x_v, d_v, u_v, v_v, rank_v, pres_v, y_v, car_tmp, car_out, car_in, rs_out, rs_in, zx_out, zx_in,
    in_sem, y_ssem, y_rsem, car_ssem, car_rsem, rs_ssem, rs_rsem, zx_ssem, zx_rsem, ag_ssem, ag_rsem, met_sem, open_sem,
):
    b = lax.axis_index("blk")
    c = lax.axis_index("col")
    barrier = pltpu.get_barrier_semaphore()

    def greet(peers):
        for peer in peers:
            pl.semaphore_signal(barrier, inc=1, device_id=peer, device_id_type=MESH)

    def load(i, src, dst):
        copy = pltpu.make_async_copy(src, dst, in_sem.at[i])
        copy.start()
        return copy

    pairs = [partners(b, c, s) for s in range(2)]
    greet([pairs[0][0], pairs[1][0], pairs[0][1], pairs[1][1]])
    small = [load(0, rank_hbm, rank_v), load(1, pres_hbm, pres_v)]
    x_load = load(2, x_hbm, x_v)
    above, below = quarter(b, c, 4), quarter(b, c, 12)
    g = lax.rem(c, HALF)
    base = c - g
    far_first = (4, 5, 3, 2, 6, 7, 1)
    ids = [lax.rem(g + o, HALF) for o in far_first]
    group = [(b, base + i) for i in ids]
    greet([above, below] + group)
    tiles = [
        [load(3 + 2 * s, u_hbm.at[:, :, s], u_v.at[:, :, s]), load(4 + 2 * s, v_hbm.at[:, :, s], v_v.at[:, :, s])]
        for s in range(2)
    ]
    d_load = load(7, d_hbm, d_v)
    across = (b, lax.rem(c + HALF, 2 * HALF))

    def remote(src, dst, ssem, rsem, device):
        return pltpu.make_async_remote_copy(
            src_ref=src, dst_ref=dst, send_sem=ssem, recv_sem=rsem, device_id=device, device_id_type=MESH
        )

    def wait_bytes(ref, sem):
        pltpu.make_async_copy(ref, ref, sem).wait()

    y_copies = [remote(x_v, y_v.at[s], y_ssem.at[s], y_rsem.at[s], pairs[s][1]) for s in range(2)]
    for copy in small:
        copy.wait()
    lane = lax.broadcasted_iota(jnp.int32, (8, 512), 1)
    row = lax.broadcasted_iota(jnp.int32, (8, 512), 0)
    lane_r = lane >> 6
    lane_q = (lane >> 5) & 1
    lane_k = (lane & 31).astype(F32)
    spread = (row == lane_r).astype(BF16)
    height = [dot((rank_v[q] * pres_v[q]).astype(F32).astype(BF16), spread) for q in range(2)]
    kept, shift = [], []
    for s in range(2):
        kept.append(lane_k < jnp.where(lane_q == 0, height[0][s : s + 1], height[1][s : s + 1]))
        shift.append(lane_q + jnp.where(b < 2 * c + 1 + s, 1, 0))

    def pick(a, step, s, rows):
        a = a.reshape(8, 8, 512)
        once, twice = pltpu.roll(a, step % 8, 1), pltpu.roll(a, 2 * step % 8, 1)
        a = jnp.where(shift[s][None] == 0, a, jnp.where(shift[s][None] == 1, once, twice))
        return jnp.where((kept[s] & (lane_r == rows))[None], a, 0.0).reshape(64, 512).astype(BF16)

    def section(ref, s):
        return ref[:, :, s].reshape(512, 512)

    x_load.wait()
    x = x_v[...]
    for s in range(2):
        tiles[s][0].wait()
        t = pick(dot_t(x, section(u_v, s)), -1, s, row + shift[s])
        tiles[s][1].wait()
        image = dot(t, section(v_v, s))
        for k in range(4):
            car_tmp[s, pl.ds(k, 64, stride=4), :] = image[:, 128 * k : 128 * k + 128]
        car_out[s] = car_tmp[s].reshape(HALF, CHUNK, 128).astype(BF16)

    pl.semaphore_wait(barrier, 6 + len(group))
    for copy in y_copies:
        copy.start()
    for s in range(2):
        pl.semaphore_signal(open_sem.at[s], inc=1, device_id=pairs[s][1], device_id_type=MESH)
    pl.semaphore_signal(met_sem, inc=1, device_id=below, device_id_type=MESH)

    d_load.wait()
    dg = dot_t(x, d_v[...]).reshape(8, 8, 256)
    dg = jnp.where((lane[:, :256] >> 5 == row[:, :256])[None], dg, 0.0).reshape(64, 256)
    dg = dg[:, :128] + dg[:, 128:]
    dg = dg + pltpu.roll(dg, 64, 1)
    dg = dg + pltpu.roll(dg, 32, 1)
    total = jnp.concatenate([dg] * 4, 1).reshape(8, 8, 512)
    total = jnp.where((lane >> 5 == c)[None], total, 0.0).reshape(64, 512)

    at_home = c == 2 * HALF - 1
    for s in range(2):
        pl.semaphore_wait(open_sem.at[s], 1)
        src_b, src_c = pairs[s][0]
        src_base = src_c - lax.rem(src_c, HALF)
        for i in ids + [g]:
            src, dst = car_out.at[s, i], car_in.at[s, g]
            copy = remote(src, dst, car_ssem, car_rsem, (src_b, src_base + i))
            if s == 1 and i is g:
                inside = pltpu.make_async_copy(src, dst, car_rsem)
                pl.when(at_home)(lambda: inside.start())
                pl.when(jnp.logical_not(at_home))(lambda: copy.start())
            else:
                copy.start()

    for s in range(2):
        y_copies[s].wait_recv()
        a = pick(dot_t(y_v[s], section(v_v, s)), 1, s, row)
        total = total + dot(a, section(u_v, s))
    for k in range(4):
        rs_out[pl.ds(k, 64, stride=4), :] = total[:, 128 * k : 128 * k + 128]

    def chunk(i):
        return pl.ds(pl.multiple_of(CHUNK * i, CHUNK), CHUNK)

    for i, peer in zip(ids, group):
        remote(rs_out.at[chunk(i)], rs_in.at[g], rs_ssem, rs_rsem, peer).start()
    rs_in[g] = rs_out[chunk(g), :]
    for copy in y_copies:
        copy.wait_send()

    wait_bytes(car_in, car_rsem)
    part = car_in[0, 0].astype(F32)
    for j in range(1, 2 * HALF):
        part = part + car_in[j // HALF, j % HALF].astype(F32)
    wait_bytes(rs_in.at[pl.ds(0, HALF - 1)], rs_rsem)
    for j in range(HALF):
        part = part + rs_in[j]
    zx_out[...] = part
    zx_copy = remote(zx_out, zx_in, zx_ssem, zx_rsem, across)
    pl.semaphore_wait(met_sem, 1)
    zx_copy.start()
    wait_bytes(rs_in.at[pl.ds(0, HALF - 1)], rs_ssem)
    wait_bytes(car_out.at[0], car_ssem)
    pl.when(at_home)(lambda: wait_bytes(car_out.at[1, pl.ds(0, HALF - 1)], car_ssem))
    pl.when(jnp.logical_not(at_home))(lambda: wait_bytes(car_out.at[1], car_ssem))

    zx_copy.wait_recv()
    mine = out.at[chunk(g)]
    mine[...] = part + zx_in[...]
    for peer in group:
        remote(mine, mine, ag_ssem, ag_rsem, peer).start()
    zx_copy.wait_send()
    others = out.at[pl.ds(0, CHUNK * (HALF - 1))]
    wait_bytes(others, ag_rsem)
    wait_bytes(others, ag_ssem)


def shards(probes, diag_tiles, left_factors, right_factors, ranks, present):
    hbm = pl.BlockSpec(memory_space=pltpu.HBM)
    dma = pltpu.SemaphoreType.DMA
    out = pl.pallas_call(
        kernel,
        out_shape=pltpu.VMEM((256, 128), F32),
        in_specs=[hbm] * 6,
        out_specs=pl.BlockSpec(memory_space=pltpu.VMEM),
        scratch_shapes=[
            pltpu.VMEM((64, 512), BF16),
            pltpu.VMEM((256, 512), BF16),
            pltpu.VMEM((8, 2, 2, 32, 512), BF16),
            pltpu.VMEM((8, 2, 2, 32, 512), BF16),
            pltpu.VMEM((2, 2, 8), jnp.int32),
            pltpu.VMEM((2, 2, 8), jnp.int32),
            pltpu.VMEM((2, 64, 512), BF16),
            pltpu.VMEM((2, 256, 128), F32),
            pltpu.VMEM((2, HALF, CHUNK, 128), BF16),
            pltpu.VMEM((2, HALF, CHUNK, 128), BF16),
            pltpu.VMEM((256, 128), F32),
            pltpu.VMEM((HALF, CHUNK, 128), F32),
            pltpu.VMEM((CHUNK, 128), F32),
            pltpu.VMEM((CHUNK, 128), F32),
            dma((8,)),
            dma((2,)),
            dma((2,)),
            dma,
            dma,
            dma,
            dma,
            dma,
            dma,
            dma,
            dma,
            pltpu.SemaphoreType.REGULAR,
            pltpu.SemaphoreType.REGULAR((2,)),
        ],
        compiler_params=pltpu.CompilerParams(
            collective_id=0, has_side_effects=True, vmem_limit_bytes=60 * 1024 * 1024
        ),
        cost_estimate=pl.CostEstimate(flops=300_000_000, bytes_accessed=2_500_000, transcendentals=0),
    )(
        probes.reshape(64, 512),
        diag_tiles.reshape(256, 512),
        left_factors[:, 0],
        right_factors[:, 0],
        jnp.transpose(ranks[:, 0], (1, 2, 0)),
        jnp.transpose(present[:, 0], (1, 2, 0)),
    )
    return out.reshape(8, 8, 1, 512)


def solution(mesh):
    return jax.shard_map(
        shards,
        mesh=mesh,
        in_specs=(
            P(None, None, "blk", None),
            P(None, "blk", "col", None),
            P(None, "blk", None, "col", None, None),
            P(None, "blk", None, "col", None, None),
            P(None, "blk", None, "col"),
            P(None, "blk", None, "col"),
        ),
        out_specs=P(None, None, "blk", None),
        check_vma=False,
    )
```

```python
import functools

import jax
import jax.numpy as jnp
from jax import lax
from jax.experimental import pallas as pl
from jax.experimental.pallas import tpu as pltpu
from jax.sharding import PartitionSpec as P

MESH = pl.DeviceIdType.MESH
BF16 = jnp.bfloat16
F32 = jnp.float32

NBLK = 32
HALF = 8
ZRING = 16
ZLOW = 8
CHUNK = 32


def dot(a, b):
    return lax.dot_general(a, b, (((1,), (0,)), ((), ())), preferred_element_type=F32)


def dot_t(a, b):
    return lax.dot_general(a, b, (((1,), (1,)), ((), ())), preferred_element_type=F32)


def partners(b, c, s):
    zl = lax.rem(b, ZLOW)
    zh = lax.div(c, HALF)
    g = lax.rem(c, HALF)
    z = zh * ZLOW + zl
    flip = g if s == 0 else g + 1 - 2 * lax.rem(g, 2)
    src_b = lax.rem(b + 2 * NBLK - (2 * c + 1 + s), NBLK)
    src_h = lax.rem(lax.div(z - lax.rem(src_b, ZLOW) + ZRING + 4, ZLOW), 2)
    shift = 2 * flip + 1 + s
    dst_h = lax.rem(lax.div(lax.rem(zl + shift, ZLOW) - z + ZRING + 4, ZLOW), 2)
    dst_b = lax.rem(b + shift + 16 * dst_h, NBLK)
    return (src_b, src_h * HALF + flip), (dst_b, dst_h * HALF + flip)


def quarter(b, c, up):
    zl = lax.rem(b, ZLOW)
    z = lax.rem(lax.div(c, HALF) * ZLOW + zl + up, ZRING)
    return b - zl + lax.rem(z, ZLOW), lax.div(z, ZLOW) * HALF + lax.rem(c, HALF)


def kernel(
    x_hbm, d_hbm, u_hbm, v_hbm, rank_hbm, pres_hbm, out,
    x_v, d_v, u_v, v_v, rank_v, pres_v, y_v, car_tmp, car_out, car_in, rs_out, rs_in, zx_out, zx_in,
    in_sem, y_ssem, y_rsem, car_ssem, car_rsem, rs_ssem, rs_rsem, zx_ssem, zx_rsem, ag_ssem, ag_rsem, met_sem, open_sem,
):
    b = lax.axis_index("blk")
    c = lax.axis_index("col")
    barrier = pltpu.get_barrier_semaphore()

    def greet(peers):
        for peer in peers:
            pl.semaphore_signal(barrier, inc=1, device_id=peer, device_id_type=MESH)

    def load(i, src, dst):
        copy = pltpu.make_async_copy(src, dst, in_sem.at[i])
        copy.start()
        return copy

    pairs = [partners(b, c, s) for s in range(2)]
    greet([pairs[0][0], pairs[1][0], pairs[0][1], pairs[1][1]])
    small = [load(0, rank_hbm, rank_v), load(1, pres_hbm, pres_v)]
    x_load = load(2, x_hbm, x_v)
    above, below = quarter(b, c, 4), quarter(b, c, 12)
    g = lax.rem(c, HALF)
    base = c - g
    far_first = (4, 5, 3, 2, 6, 7, 1)
    ids = [lax.rem(g + o, HALF) for o in far_first]
    group = [(b, base + i) for i in ids]
    greet([above, below] + group)
    tiles = [
        [load(3 + 2 * s, u_hbm.at[:, :, s], u_v.at[:, :, s]), load(4 + 2 * s, v_hbm.at[:, :, s], v_v.at[:, :, s])]
        for s in range(2)
    ]
    d_load = load(7, d_hbm, d_v)
    across = (b, lax.rem(c + HALF, 2 * HALF))

    def remote(src, dst, ssem, rsem, device):
        return pltpu.make_async_remote_copy(
            src_ref=src, dst_ref=dst, send_sem=ssem, recv_sem=rsem, device_id=device, device_id_type=MESH
        )

    def wait_bytes(ref, sem):
        pltpu.make_async_copy(ref, ref, sem).wait()

    y_copies = [remote(x_v, y_v.at[s], y_ssem.at[s], y_rsem.at[s], pairs[s][1]) for s in range(2)]
    for copy in small:
        copy.wait()
    lane = lax.broadcasted_iota(jnp.int32, (8, 512), 1)
    row = lax.broadcasted_iota(jnp.int32, (8, 512), 0)
    lane_r = lane >> 6
    lane_q = (lane >> 5) & 1
    lane_k = (lane & 31).astype(F32)
    spread = (row == lane_r).astype(BF16)
    height = [dot((rank_v[q] * pres_v[q]).astype(F32).astype(BF16), spread) for q in range(2)]
    kept, shift = [], []
    for s in range(2):
        kept.append(lane_k < jnp.where(lane_q == 0, height[0][s : s + 1], height[1][s : s + 1]))
        shift.append(lane_q + jnp.where(b < 2 * c + 1 + s, 1, 0))

    def pick(a, step, s, rows):
        a = a.reshape(8, 8, 512)
        once, twice = pltpu.roll(a, step % 8, 1), pltpu.roll(a, 2 * step % 8, 1)
        a = jnp.where(shift[s][None] == 0, a, jnp.where(shift[s][None] == 1, once, twice))
        return jnp.where((kept[s] & (lane_r == rows))[None], a, 0.0).reshape(64, 512).astype(BF16)

    def section(ref, s):
        return ref[:, :, s].reshape(512, 512)

    x_load.wait()
    x = x_v[...]
    for s in range(2):
        tiles[s][0].wait()
        t = pick(dot_t(x, section(u_v, s)), -1, s, row + shift[s])
        tiles[s][1].wait()
        image = dot(t, section(v_v, s))
        for k in range(4):
            car_tmp[s, pl.ds(k, 64, stride=4), :] = image[:, 128 * k : 128 * k + 128]
        car_out[s] = car_tmp[s].reshape(HALF, CHUNK, 128).astype(BF16)

    pl.semaphore_wait(barrier, 6 + len(group))
    for s in range(2):
        pl.semaphore_signal(open_sem.at[s], inc=1, device_id=pairs[s][1], device_id_type=MESH)
    for copy in y_copies:
        copy.start()
    pl.semaphore_signal(met_sem, inc=1, device_id=below, device_id_type=MESH)

    d_load.wait()
    dg = dot_t(x, d_v[...]).reshape(8, 8, 256)
    dg = jnp.where((lane[:, :256] >> 5 == row[:, :256])[None], dg, 0.0).reshape(64, 256)
    dg = dg[:, :128] + dg[:, 128:]
    dg = dg + pltpu.roll(dg, 64, 1)
    dg = dg + pltpu.roll(dg, 32, 1)
    total = jnp.concatenate([dg] * 4, 1).reshape(8, 8, 512)
    total = jnp.where((lane >> 5 == c)[None], total, 0.0).reshape(64, 512)

    at_home = c == 2 * HALF - 1
    for s in range(2):
        pl.semaphore_wait(open_sem.at[s], 1)
    bases = [pairs[s][0][1] - lax.rem(pairs[s][0][1], HALF) for s in range(2)]
    for i in ids + [g]:
        for s in range(2):
            src, dst = car_out.at[s, i], car_in.at[s, g]
            copy = remote(src, dst, car_ssem, car_rsem, (pairs[s][0][0], bases[s] + i))
            if s == 1 and i is g:
                inside = pltpu.make_async_copy(src, dst, car_rsem)
                pl.when(at_home)(lambda: inside.start())
                pl.when(jnp.logical_not(at_home))(lambda: copy.start())
            else:
                copy.start()

    for s in range(2):
        y_copies[s].wait_recv()
        a = pick(dot_t(y_v[s], section(v_v, s)), 1, s, row)
        total = total + dot(a, section(u_v, s))
    for k in range(4):
        rs_out[pl.ds(k, 64, stride=4), :] = total[:, 128 * k : 128 * k + 128]

    def chunk(i):
        return pl.ds(pl.multiple_of(CHUNK * i, CHUNK), CHUNK)

    for i, peer in zip(ids, group):
        remote(rs_out.at[chunk(i)], rs_in.at[g], rs_ssem, rs_rsem, peer).start()
    rs_in[g] = rs_out[chunk(g), :]
    for copy in y_copies:
        copy.wait_send()

    wait_bytes(car_in, car_rsem)
    part = car_in[0, 0].astype(F32)
    for j in range(1, 2 * HALF):
        part = part + car_in[j // HALF, j % HALF].astype(F32)
    wait_bytes(rs_in.at[pl.ds(0, HALF - 1)], rs_rsem)
    for j in range(HALF):
        part = part + rs_in[j]
    zx_out[...] = part
    zx_copy = remote(zx_out, zx_in, zx_ssem, zx_rsem, across)
    pl.semaphore_wait(met_sem, 1)
    zx_copy.start()
    wait_bytes(rs_in.at[pl.ds(0, HALF - 1)], rs_ssem)
    wait_bytes(car_out.at[0], car_ssem)
    pl.when(at_home)(lambda: wait_bytes(car_out.at[1, pl.ds(0, HALF - 1)], car_ssem))
    pl.when(jnp.logical_not(at_home))(lambda: wait_bytes(car_out.at[1], car_ssem))

    zx_copy.wait_recv()
    mine = out.at[chunk(g)]
    mine[...] = part + zx_in[...]
    for peer in group:
        remote(mine, mine, ag_ssem, ag_rsem, peer).start()
    zx_copy.wait_send()
    others = out.at[pl.ds(0, CHUNK * (HALF - 1))]
    wait_bytes(others, ag_rsem)
    wait_bytes(others, ag_ssem)


def shards(probes, diag_tiles, left_factors, right_factors, ranks, present):
    hbm = pl.BlockSpec(memory_space=pltpu.HBM)
    dma = pltpu.SemaphoreType.DMA
    out = pl.pallas_call(
        kernel,
        out_shape=pltpu.VMEM((256, 128), F32),
        in_specs=[hbm] * 6,
        out_specs=pl.BlockSpec(memory_space=pltpu.VMEM),
        scratch_shapes=[
            pltpu.VMEM((64, 512), BF16),
            pltpu.VMEM((256, 512), BF16),
            pltpu.VMEM((8, 2, 2, 32, 512), BF16),
            pltpu.VMEM((8, 2, 2, 32, 512), BF16),
            pltpu.VMEM((2, 2, 8), jnp.int32),
            pltpu.VMEM((2, 2, 8), jnp.int32),
            pltpu.VMEM((2, 64, 512), BF16),
            pltpu.VMEM((2, 256, 128), F32),
            pltpu.VMEM((2, HALF, CHUNK, 128), BF16),
            pltpu.VMEM((2, HALF, CHUNK, 128), BF16),
            pltpu.VMEM((256, 128), F32),
            pltpu.VMEM((HALF, CHUNK, 128), F32),
            pltpu.VMEM((CHUNK, 128), F32),
            pltpu.VMEM((CHUNK, 128), F32),
            dma((8,)),
            dma((2,)),
            dma((2,)),
            dma,
            dma,
            dma,
            dma,
            dma,
            dma,
            dma,
            dma,
            pltpu.SemaphoreType.REGULAR,
            pltpu.SemaphoreType.REGULAR((2,)),
        ],
        compiler_params=pltpu.CompilerParams(
            collective_id=0, has_side_effects=True, vmem_limit_bytes=60 * 1024 * 1024
        ),
        cost_estimate=pl.CostEstimate(flops=300_000_000, bytes_accessed=2_500_000, transcendentals=0),
    )(
        probes.reshape(64, 512),
        diag_tiles.reshape(256, 512),
        left_factors[:, 0],
        right_factors[:, 0],
        jnp.transpose(ranks[:, 0], (1, 2, 0)),
        jnp.transpose(present[:, 0], (1, 2, 0)),
    )
    return out.reshape(8, 8, 1, 512)


def solution(mesh):
    return jax.shard_map(
        shards,
        mesh=mesh,
        in_specs=(
            P(None, None, "blk", None),
            P(None, "blk", "col", None),
            P(None, "blk", None, "col", None, None),
            P(None, "blk", None, "col", None, None),
            P(None, "blk", None, "col"),
            P(None, "blk", None, "col"),
        ),
        out_specs=P(None, None, "blk", None),
        check_vma=False,
    )
```

```python
import functools

import jax
import jax.numpy as jnp
from jax import lax
from jax.experimental import pallas as pl
from jax.experimental.pallas import tpu as pltpu
from jax.sharding import PartitionSpec as P

MESH = pl.DeviceIdType.MESH
BF16 = jnp.bfloat16
F32 = jnp.float32

NBLK = 32
HALF = 8
ZRING = 16
ZLOW = 8
CHUNK = 32


def dot(a, b):
    return lax.dot_general(a, b, (((1,), (0,)), ((), ())), preferred_element_type=F32)


def dot_t(a, b):
    return lax.dot_general(a, b, (((1,), (1,)), ((), ())), preferred_element_type=F32)


def partners(b, c, s):
    zl = lax.rem(b, ZLOW)
    zh = lax.div(c, HALF)
    g = lax.rem(c, HALF)
    z = zh * ZLOW + zl
    flip = g if s == 0 else g + 1 - 2 * lax.rem(g, 2)
    src_b = lax.rem(b + 2 * NBLK - (2 * c + 1 + s), NBLK)
    src_h = lax.rem(lax.div(z - lax.rem(src_b, ZLOW) + ZRING + 4, ZLOW), 2)
    shift = 2 * flip + 1 + s
    dst_h = lax.rem(lax.div(lax.rem(zl + shift, ZLOW) - z + ZRING + 4, ZLOW), 2)
    dst_b = lax.rem(b + shift + 16 * dst_h, NBLK)
    return (src_b, src_h * HALF + flip), (dst_b, dst_h * HALF + flip)


def quarter(b, c, up):
    zl = lax.rem(b, ZLOW)
    z = lax.rem(lax.div(c, HALF) * ZLOW + zl + up, ZRING)
    return b - zl + lax.rem(z, ZLOW), lax.div(z, ZLOW) * HALF + lax.rem(c, HALF)


def kernel(
    x_hbm, d_hbm, u_hbm, v_hbm, rank_hbm, pres_hbm, out,
    x_v, d_v, u_v, v_v, rank_v, pres_v, y_v, car_tmp, car_out, car_in, rs_out, rs_in, zx_out, zx_in,
    in_sem, y_ssem, y_rsem, car_ssem, car_rsem, rs_ssem, rs_rsem, zx_ssem, zx_rsem, ag_ssem, ag_rsem, met_sem, open_sem,
):
    b = lax.axis_index("blk")
    c = lax.axis_index("col")
    barrier = pltpu.get_barrier_semaphore()

    def greet(peers):
        for peer in peers:
            pl.semaphore_signal(barrier, inc=1, device_id=peer, device_id_type=MESH)

    def load(i, src, dst):
        copy = pltpu.make_async_copy(src, dst, in_sem.at[i])
        copy.start()
        return copy

    pairs = [partners(b, c, s) for s in range(2)]
    greet([pairs[0][0], pairs[1][0]])
    small = [load(0, rank_hbm, rank_v), load(1, pres_hbm, pres_v)]
    x_load = load(2, x_hbm, x_v)
    above, below = quarter(b, c, 4), quarter(b, c, 12)
    g = lax.rem(c, HALF)
    base = c - g
    far_first = (4, 5, 3, 2, 6, 7, 1)
    ids = [lax.rem(g + o, HALF) for o in far_first]
    group = [(b, base + i) for i in ids]
    greet([above, below] + group)
    tiles = [
        [load(3 + 2 * s, u_hbm.at[:, :, s], u_v.at[:, :, s]), load(4 + 2 * s, v_hbm.at[:, :, s], v_v.at[:, :, s])]
        for s in range(2)
    ]
    d_load = load(7, d_hbm, d_v)
    across = (b, lax.rem(c + HALF, 2 * HALF))

    def remote(src, dst, ssem, rsem, device):
        return pltpu.make_async_remote_copy(
            src_ref=src, dst_ref=dst, send_sem=ssem, recv_sem=rsem, device_id=device, device_id_type=MESH
        )

    def wait_bytes(ref, sem):
        pltpu.make_async_copy(ref, ref, sem).wait()

    y_copies = [remote(x_v, y_v.at[s], y_ssem.at[s], y_rsem.at[s], pairs[s][1]) for s in range(2)]
    for copy in small:
        copy.wait()
    lane = lax.broadcasted_iota(jnp.int32, (8, 512), 1)
    row = lax.broadcasted_iota(jnp.int32, (8, 512), 0)
    lane_r = lane >> 6
    lane_q = (lane >> 5) & 1
    lane_k = (lane & 31).astype(F32)
    spread = (row == lane_r).astype(BF16)
    height = [dot((rank_v[q] * pres_v[q]).astype(F32).astype(BF16), spread) for q in range(2)]
    kept, shift = [], []
    for s in range(2):
        kept.append(lane_k < jnp.where(lane_q == 0, height[0][s : s + 1], height[1][s : s + 1]))
        shift.append(lane_q + jnp.where(b < 2 * c + 1 + s, 1, 0))

    def pick(a, step, s, rows):
        a = a.reshape(8, 8, 512)
        once, twice = pltpu.roll(a, step % 8, 1), pltpu.roll(a, 2 * step % 8, 1)
        a = jnp.where(shift[s][None] == 0, a, jnp.where(shift[s][None] == 1, once, twice))
        return jnp.where((kept[s] & (lane_r == rows))[None], a, 0.0).reshape(64, 512).astype(BF16)

    def section(ref, s):
        return ref[:, :, s].reshape(512, 512)

    x_load.wait()
    x = x_v[...]
    for s in range(2):
        tiles[s][0].wait()
        t = pick(dot_t(x, section(u_v, s)), -1, s, row + shift[s])
        tiles[s][1].wait()
        image = dot(t, section(v_v, s))
        for k in range(4):
            car_tmp[s, pl.ds(k, 64, stride=4), :] = image[:, 128 * k : 128 * k + 128]
        car_out[s] = car_tmp[s].reshape(HALF, CHUNK, 128).astype(BF16)

    pl.semaphore_wait(barrier, 4 + len(group))
    for s in range(2):
        pl.semaphore_signal(open_sem.at[s], inc=1, device_id=pairs[s][1], device_id_type=MESH)
    for copy in y_copies:
        copy.start()
    pl.semaphore_signal(met_sem, inc=1, device_id=below, device_id_type=MESH)

    d_load.wait()
    dg = dot_t(x, d_v[...]).reshape(8, 8, 256)
    dg = jnp.where((lane[:, :256] >> 5 == row[:, :256])[None], dg, 0.0).reshape(64, 256)
    dg = dg[:, :128] + dg[:, 128:]
    dg = dg + pltpu.roll(dg, 64, 1)
    dg = dg + pltpu.roll(dg, 32, 1)
    total = jnp.concatenate([dg] * 4, 1).reshape(8, 8, 512)
    total = jnp.where((lane >> 5 == c)[None], total, 0.0).reshape(64, 512)

    at_home = c == 2 * HALF - 1
    for s in range(2):
        pl.semaphore_wait(open_sem.at[s], 1)
    bases = [pairs[s][0][1] - lax.rem(pairs[s][0][1], HALF) for s in range(2)]
    for i in ids + [g]:
        for s in range(2):
            src, dst = car_out.at[s, i], car_in.at[s, g]
            copy = remote(src, dst, car_ssem, car_rsem, (pairs[s][0][0], bases[s] + i))
            if s == 1 and i is g:
                inside = pltpu.make_async_copy(src, dst, car_rsem)
                pl.when(at_home)(lambda: inside.start())
                pl.when(jnp.logical_not(at_home))(lambda: copy.start())
            else:
                copy.start()

    for s in range(2):
        y_copies[s].wait_recv()
        a = pick(dot_t(y_v[s], section(v_v, s)), 1, s, row)
        total = total + dot(a, section(u_v, s))
    for k in range(4):
        rs_out[pl.ds(k, 64, stride=4), :] = total[:, 128 * k : 128 * k + 128]

    def chunk(i):
        return pl.ds(pl.multiple_of(CHUNK * i, CHUNK), CHUNK)

    for i, peer in zip(ids, group):
        remote(rs_out.at[chunk(i)], rs_in.at[g], rs_ssem, rs_rsem, peer).start()
    rs_in[g] = rs_out[chunk(g), :]
    for copy in y_copies:
        copy.wait_send()

    wait_bytes(car_in, car_rsem)
    part = car_in[0, 0].astype(F32)
    for j in range(1, 2 * HALF):
        part = part + car_in[j // HALF, j % HALF].astype(F32)
    wait_bytes(rs_in.at[pl.ds(0, HALF - 1)], rs_rsem)
    for j in range(HALF):
        part = part + rs_in[j]
    zx_out[...] = part
    zx_copy = remote(zx_out, zx_in, zx_ssem, zx_rsem, across)
    pl.semaphore_wait(met_sem, 1)
    zx_copy.start()
    wait_bytes(rs_in.at[pl.ds(0, HALF - 1)], rs_ssem)
    wait_bytes(car_out.at[0], car_ssem)
    pl.when(at_home)(lambda: wait_bytes(car_out.at[1, pl.ds(0, HALF - 1)], car_ssem))
    pl.when(jnp.logical_not(at_home))(lambda: wait_bytes(car_out.at[1], car_ssem))

    zx_copy.wait_recv()
    mine = out.at[chunk(g)]
    mine[...] = part + zx_in[...]
    for peer in group:
        remote(mine, mine, ag_ssem, ag_rsem, peer).start()
    zx_copy.wait_send()
    others = out.at[pl.ds(0, CHUNK * (HALF - 1))]
    wait_bytes(others, ag_rsem)
    wait_bytes(others, ag_ssem)


def shards(probes, diag_tiles, left_factors, right_factors, ranks, present):
    hbm = pl.BlockSpec(memory_space=pltpu.HBM)
    dma = pltpu.SemaphoreType.DMA
    out = pl.pallas_call(
        kernel,
        out_shape=pltpu.VMEM((256, 128), F32),
        in_specs=[hbm] * 6,
        out_specs=pl.BlockSpec(memory_space=pltpu.VMEM),
        scratch_shapes=[
            pltpu.VMEM((64, 512), BF16),
            pltpu.VMEM((256, 512), BF16),
            pltpu.VMEM((8, 2, 2, 32, 512), BF16),
            pltpu.VMEM((8, 2, 2, 32, 512), BF16),
            pltpu.VMEM((2, 2, 8), jnp.int32),
            pltpu.VMEM((2, 2, 8), jnp.int32),
            pltpu.VMEM((2, 64, 512), BF16),
            pltpu.VMEM((2, 256, 128), F32),
            pltpu.VMEM((2, HALF, CHUNK, 128), BF16),
            pltpu.VMEM((2, HALF, CHUNK, 128), BF16),
            pltpu.VMEM((256, 128), F32),
            pltpu.VMEM((HALF, CHUNK, 128), F32),
            pltpu.VMEM((CHUNK, 128), F32),
            pltpu.VMEM((CHUNK, 128), F32),
            dma((8,)),
            dma((2,)),
            dma((2,)),
            dma,
            dma,
            dma,
            dma,
            dma,
            dma,
            dma,
            dma,
            pltpu.SemaphoreType.REGULAR,
            pltpu.SemaphoreType.REGULAR((2,)),
        ],
        compiler_params=pltpu.CompilerParams(
            collective_id=0, has_side_effects=True, vmem_limit_bytes=60 * 1024 * 1024
        ),
        cost_estimate=pl.CostEstimate(flops=300_000_000, bytes_accessed=2_500_000, transcendentals=0),
    )(
        probes.reshape(64, 512),
        diag_tiles.reshape(256, 512),
        left_factors[:, 0],
        right_factors[:, 0],
        jnp.transpose(ranks[:, 0], (1, 2, 0)),
        jnp.transpose(present[:, 0], (1, 2, 0)),
    )
    return out.reshape(8, 8, 1, 512)


def solution(mesh):
    return jax.shard_map(
        shards,
        mesh=mesh,
        in_specs=(
            P(None, None, "blk", None),
            P(None, "blk", "col", None),
            P(None, "blk", None, "col", None, None),
            P(None, "blk", None, "col", None, None),
            P(None, "blk", None, "col"),
            P(None, "blk", None, "col"),
        ),
        out_specs=P(None, None, "blk", None),
        check_vma=False,
    )
```

```python
import functools

import jax
import jax.numpy as jnp
from jax import lax
from jax.experimental import pallas as pl
from jax.experimental.pallas import tpu as pltpu
from jax.sharding import PartitionSpec as P

MESH = pl.DeviceIdType.MESH
BF16 = jnp.bfloat16
F32 = jnp.float32

NBLK = 32
HALF = 8
ZRING = 16
ZLOW = 8
CHUNK = 32


def dot(a, b):
    return lax.dot_general(a, b, (((1,), (0,)), ((), ())), preferred_element_type=F32)


def dot_t(a, b):
    return lax.dot_general(a, b, (((1,), (1,)), ((), ())), preferred_element_type=F32)


def partners(b, c, s):
    zl = lax.rem(b, ZLOW)
    zh = lax.div(c, HALF)
    g = lax.rem(c, HALF)
    z = zh * ZLOW + zl
    flip = g if s == 0 else g + 1 - 2 * lax.rem(g, 2)
    src_b = lax.rem(b + 2 * NBLK - (2 * c + 1 + s), NBLK)
    src_h = lax.rem(lax.div(z - lax.rem(src_b, ZLOW) + ZRING + 4, ZLOW), 2)
    shift = 2 * flip + 1 + s
    dst_h = lax.rem(lax.div(lax.rem(zl + shift, ZLOW) - z + ZRING + 4, ZLOW), 2)
    dst_b = lax.rem(b + shift + 16 * dst_h, NBLK)
    return (src_b, src_h * HALF + flip), (dst_b, dst_h * HALF + flip)


def quarter(b, c, up):
    zl = lax.rem(b, ZLOW)
    z = lax.rem(lax.div(c, HALF) * ZLOW + zl + up, ZRING)
    return b - zl + lax.rem(z, ZLOW), lax.div(z, ZLOW) * HALF + lax.rem(c, HALF)


def kernel(
    x_hbm, d_hbm, u_hbm, v_hbm, rank_hbm, pres_hbm, out,
    x_v, d_v, u_v, v_v, rank_v, pres_v, y_v, car_tmp, car_out, car_in, rs_out, rs_in, zx_out, zx_in,
    in_sem, y_ssem, y_rsem, car_ssem, car_rsem, rs_ssem, rs_rsem, zx_ssem, zx_rsem, ag_ssem, ag_rsem, met_sem, open_sem,
):
    b = lax.axis_index("blk")
    c = lax.axis_index("col")
    barrier = pltpu.get_barrier_semaphore()

    def greet(peers):
        for peer in peers:
            pl.semaphore_signal(barrier, inc=1, device_id=peer, device_id_type=MESH)

    def load(i, src, dst):
        copy = pltpu.make_async_copy(src, dst, in_sem.at[i])
        copy.start()
        return copy

    pairs = [partners(b, c, s) for s in range(2)]
    greet([pairs[0][0], pairs[1][0]])
    small = [load(0, rank_hbm, rank_v), load(1, pres_hbm, pres_v)]
    x_load = load(2, x_hbm, x_v)
    above, below = quarter(b, c, 4), quarter(b, c, 12)
    g = lax.rem(c, HALF)
    base = c - g

    def others_in_half(step):
        def one(k, carry):
            step(lax.rem(g + 1 + lax.rem(k + 3, HALF - 1), HALF))
            return carry

        lax.fori_loop(0, HALF - 1, one, 0)

    greet([above, below])
    others_in_half(lambda i: greet([(b, base + i)]))
    tiles = [
        [load(3 + 2 * s, u_hbm.at[:, :, s], u_v.at[:, :, s]), load(4 + 2 * s, v_hbm.at[:, :, s], v_v.at[:, :, s])]
        for s in range(2)
    ]
    d_load = load(7, d_hbm, d_v)
    across = (b, lax.rem(c + HALF, 2 * HALF))

    def remote(src, dst, ssem, rsem, device):
        return pltpu.make_async_remote_copy(
            src_ref=src, dst_ref=dst, send_sem=ssem, recv_sem=rsem, device_id=device, device_id_type=MESH
        )

    def wait_bytes(ref, sem):
        pltpu.make_async_copy(ref, ref, sem).wait()

    y_copies = [remote(x_v, y_v.at[s], y_ssem.at[s], y_rsem.at[s], pairs[s][1]) for s in range(2)]
    for copy in small:
        copy.wait()
    lane = lax.broadcasted_iota(jnp.int32, (8, 512), 1)
    row = lax.broadcasted_iota(jnp.int32, (8, 512), 0)
    lane_r = lane >> 6
    lane_q = (lane >> 5) & 1
    lane_k = (lane & 31).astype(F32)
    spread = (row == lane_r).astype(BF16)
    height = [dot((rank_v[q] * pres_v[q]).astype(F32).astype(BF16), spread) for q in range(2)]
    kept, shift = [], []
    for s in range(2):
        kept.append(lane_k < jnp.where(lane_q == 0, height[0][s : s + 1], height[1][s : s + 1]))
        shift.append(lane_q + jnp.where(b < 2 * c + 1 + s, 1, 0))

    def pick(a, step, s, rows):
        a = a.reshape(8, 8, 512)
        once, twice = pltpu.roll(a, step % 8, 1), pltpu.roll(a, 2 * step % 8, 1)
        a = jnp.where(shift[s][None] == 0, a, jnp.where(shift[s][None] == 1, once, twice))
        return jnp.where((kept[s] & (lane_r == rows))[None], a, 0.0).reshape(64, 512).astype(BF16)

    def section(ref, s):
        return ref[:, :, s].reshape(512, 512)

    x_load.wait()
    x = x_v[...]
    for s in range(2):
        tiles[s][0].wait()
        t = pick(dot_t(x, section(u_v, s)), -1, s, row + shift[s])
        tiles[s][1].wait()
        image = dot(t, section(v_v, s))
        for k in range(4):
            car_tmp[s, pl.ds(k, 64, stride=4), :] = image[:, 128 * k : 128 * k + 128]
        car_out[s] = car_tmp[s].reshape(HALF, CHUNK, 128).astype(BF16)

    pl.semaphore_wait(barrier, 4 + HALF - 1)
    for s in range(2):
        pl.semaphore_signal(open_sem.at[s], inc=1, device_id=pairs[s][1], device_id_type=MESH)
    for copy in y_copies:
        copy.start()
    pl.semaphore_signal(met_sem, inc=1, device_id=below, device_id_type=MESH)

    d_load.wait()
    dg = dot_t(x, d_v[...]).reshape(8, 8, 256)
    dg = jnp.where((lane[:, :256] >> 5 == row[:, :256])[None], dg, 0.0).reshape(64, 256)
    dg = dg[:, :128] + dg[:, 128:]
    dg = dg + pltpu.roll(dg, 64, 1)
    dg = dg + pltpu.roll(dg, 32, 1)
    total = jnp.concatenate([dg] * 4, 1).reshape(8, 8, 512)
    total = jnp.where((lane >> 5 == c)[None], total, 0.0).reshape(64, 512)

    at_home = c == 2 * HALF - 1
    for s in range(2):
        pl.semaphore_wait(open_sem.at[s], 1)
    bases = [pairs[s][0][1] - lax.rem(pairs[s][0][1], HALF) for s in range(2)]

    def scatter(i, own):
        for s in range(2):
            src, dst = car_out.at[s, i], car_in.at[s, g]
            copy = remote(src, dst, car_ssem, car_rsem, (pairs[s][0][0], bases[s] + i))
            if s == 1 and own:
                inside = pltpu.make_async_copy(src, dst, car_rsem)
                pl.when(at_home)(lambda: inside.start())
                pl.when(jnp.logical_not(at_home))(lambda: copy.start())
            else:
                copy.start()

    others_in_half(lambda i: scatter(i, False))
    scatter(g, True)

    for s in range(2):
        y_copies[s].wait_recv()
        a = pick(dot_t(y_v[s], section(v_v, s)), 1, s, row)
        total = total + dot(a, section(u_v, s))
    for k in range(4):
        rs_out[pl.ds(k, 64, stride=4), :] = total[:, 128 * k : 128 * k + 128]

    def chunk(i):
        return pl.ds(pl.multiple_of(CHUNK * i, CHUNK), CHUNK)

    others_in_half(lambda i: remote(rs_out.at[chunk(i)], rs_in.at[g], rs_ssem, rs_rsem, (b, base + i)).start())
    rs_in[g] = rs_out[chunk(g), :]
    for copy in y_copies:
        copy.wait_send()

    wait_bytes(car_in, car_rsem)
    part = car_in[0, 0].astype(F32)
    for j in range(1, 2 * HALF):
        part = part + car_in[j // HALF, j % HALF].astype(F32)
    wait_bytes(rs_in.at[pl.ds(0, HALF - 1)], rs_rsem)
    for j in range(HALF):
        part = part + rs_in[j]
    zx_out[...] = part
    zx_copy = remote(zx_out, zx_in, zx_ssem, zx_rsem, across)
    pl.semaphore_wait(met_sem, 1)
    zx_copy.start()
    wait_bytes(rs_in.at[pl.ds(0, HALF - 1)], rs_ssem)
    wait_bytes(car_out.at[0], car_ssem)
    pl.when(at_home)(lambda: wait_bytes(car_out.at[1, pl.ds(0, HALF - 1)], car_ssem))
    pl.when(jnp.logical_not(at_home))(lambda: wait_bytes(car_out.at[1], car_ssem))

    zx_copy.wait_recv()
    mine = out.at[chunk(g)]
    mine[...] = part + zx_in[...]
    others_in_half(lambda i: remote(mine, mine, ag_ssem, ag_rsem, (b, base + i)).start())
    zx_copy.wait_send()
    others = out.at[pl.ds(0, CHUNK * (HALF - 1))]
    wait_bytes(others, ag_rsem)
    wait_bytes(others, ag_ssem)


def shards(probes, diag_tiles, left_factors, right_factors, ranks, present):
    hbm = pl.BlockSpec(memory_space=pltpu.HBM)
    dma = pltpu.SemaphoreType.DMA
    out = pl.pallas_call(
        kernel,
        out_shape=pltpu.VMEM((256, 128), F32),
        in_specs=[hbm] * 6,
        out_specs=pl.BlockSpec(memory_space=pltpu.VMEM),
        scratch_shapes=[
            pltpu.VMEM((64, 512), BF16),
            pltpu.VMEM((256, 512), BF16),
            pltpu.VMEM((8, 2, 2, 32, 512), BF16),
            pltpu.VMEM((8, 2, 2, 32, 512), BF16),
            pltpu.VMEM((2, 2, 8), jnp.int32),
            pltpu.VMEM((2, 2, 8), jnp.int32),
            pltpu.VMEM((2, 64, 512), BF16),
            pltpu.VMEM((2, 256, 128), F32),
            pltpu.VMEM((2, HALF, CHUNK, 128), BF16),
            pltpu.VMEM((2, HALF, CHUNK, 128), BF16),
            pltpu.VMEM((256, 128), F32),
            pltpu.VMEM((HALF, CHUNK, 128), F32),
            pltpu.VMEM((CHUNK, 128), F32),
            pltpu.VMEM((CHUNK, 128), F32),
            dma((8,)),
            dma((2,)),
            dma((2,)),
            dma,
            dma,
            dma,
            dma,
            dma,
            dma,
            dma,
            dma,
            pltpu.SemaphoreType.REGULAR,
            pltpu.SemaphoreType.REGULAR((2,)),
        ],
        compiler_params=pltpu.CompilerParams(
            collective_id=0, has_side_effects=True, vmem_limit_bytes=60 * 1024 * 1024
        ),
        cost_estimate=pl.CostEstimate(flops=300_000_000, bytes_accessed=2_500_000, transcendentals=0),
    )(
        probes.reshape(64, 512),
        diag_tiles.reshape(256, 512),
        left_factors[:, 0],
        right_factors[:, 0],
        jnp.transpose(ranks[:, 0], (1, 2, 0)),
        jnp.transpose(present[:, 0], (1, 2, 0)),
    )
    return out.reshape(8, 8, 1, 512)


def solution(mesh):
    return jax.shard_map(
        shards,
        mesh=mesh,
        in_specs=(
            P(None, None, "blk", None),
            P(None, "blk", "col", None),
            P(None, "blk", None, "col", None, None),
            P(None, "blk", None, "col", None, None),
            P(None, "blk", None, "col"),
            P(None, "blk", None, "col"),
        ),
        out_specs=P(None, None, "blk", None),
        check_vma=False,
    )
```

```python
import functools

import jax
import jax.numpy as jnp
from jax import lax
from jax.experimental import pallas as pl
from jax.experimental.pallas import tpu as pltpu
from jax.sharding import PartitionSpec as P

MESH = pl.DeviceIdType.MESH
BF16 = jnp.bfloat16
F32 = jnp.float32

NBLK = 32
HALF = 8
ZRING = 16
ZLOW = 8
CHUNK = 32


def dot(a, b):
    return lax.dot_general(a, b, (((1,), (0,)), ((), ())), preferred_element_type=F32)


def dot_t(a, b):
    return lax.dot_general(a, b, (((1,), (1,)), ((), ())), preferred_element_type=F32)


def partners(b, c, s):
    zl = lax.rem(b, ZLOW)
    zh = lax.div(c, HALF)
    g = lax.rem(c, HALF)
    z = zh * ZLOW + zl
    flip = g if s == 0 else g + 1 - 2 * lax.rem(g, 2)
    src_b = lax.rem(b + 2 * NBLK - (2 * c + 1 + s), NBLK)
    src_h = lax.rem(lax.div(z - lax.rem(src_b, ZLOW) + ZRING + 4, ZLOW), 2)
    shift = 2 * flip + 1 + s
    dst_h = lax.rem(lax.div(lax.rem(zl + shift, ZLOW) - z + ZRING + 4, ZLOW), 2)
    dst_b = lax.rem(b + shift + 16 * dst_h, NBLK)
    return (src_b, src_h * HALF + flip), (dst_b, dst_h * HALF + flip)


def quarter(b, c, up):
    zl = lax.rem(b, ZLOW)
    z = lax.rem(lax.div(c, HALF) * ZLOW + zl + up, ZRING)
    return b - zl + lax.rem(z, ZLOW), lax.div(z, ZLOW) * HALF + lax.rem(c, HALF)


def kernel(
    x_hbm, d_hbm, u_hbm, v_hbm, rank_hbm, pres_hbm, out,
    x_v, d_v, u_v, v_v, rank_v, pres_v, y_v, car_tmp, car_out, car_in, rs_out, rs_in, zx_out, zx_in,
    in_sem, y_ssem, y_rsem, car_ssem, car_rsem, rs_ssem, rs_rsem, zx_ssem, zx_rsem, ag_ssem, ag_rsem, met_sem, open_sem,
):
    b = lax.axis_index("blk")
    c = lax.axis_index("col")
    barrier = pltpu.get_barrier_semaphore()

    def greet(peers):
        for peer in peers:
            pl.semaphore_signal(barrier, inc=1, device_id=peer, device_id_type=MESH)

    def load(i, src, dst):
        copy = pltpu.make_async_copy(src, dst, in_sem.at[i])
        copy.start()
        return copy

    pairs = [partners(b, c, s) for s in range(2)]
    greet([pairs[0][0], pairs[1][0]])
    small = [load(0, rank_hbm, rank_v), load(1, pres_hbm, pres_v)]
    x_load = load(2, x_hbm, x_v)
    above, below = quarter(b, c, 4), quarter(b, c, 12)
    g = lax.rem(c, HALF)
    base = c - g
    far_first = (4, 5, 3, 2, 6, 7, 1)
    ids = [lax.rem(g + o, HALF) for o in far_first]
    group = [(b, base + i) for i in ids]
    greet([above, below] + group)
    tiles = [
        [load(3 + 2 * s, u_hbm.at[:, :, s], u_v.at[:, :, s]), load(4 + 2 * s, v_hbm.at[:, :, s], v_v.at[:, :, s])]
        for s in range(2)
    ]
    d_load = load(7, d_hbm, d_v)
    across = (b, lax.rem(c + HALF, 2 * HALF))

    def remote(src, dst, ssem, rsem, device):
        return pltpu.make_async_remote_copy(
            src_ref=src, dst_ref=dst, send_sem=ssem, recv_sem=rsem, device_id=device, device_id_type=MESH
        )

    def wait_bytes(ref, sem):
        pltpu.make_async_copy(ref, ref, sem).wait()

    y_copies = [remote(x_v, y_v.at[s], y_ssem.at[s], y_rsem.at[s], pairs[s][1]) for s in range(2)]
    for copy in small:
        copy.wait()
    lane = lax.broadcasted_iota(jnp.int32, (8, 512), 1)
    row = lax.broadcasted_iota(jnp.int32, (8, 512), 0)
    lane_r = lane >> 6
    lane_q = (lane >> 5) & 1
    lane_k = (lane & 31).astype(F32)
    spread = (row == lane_r).astype(BF16)
    height = [dot((rank_v[q] * pres_v[q]).astype(F32).astype(BF16), spread) for q in range(2)]
    kept, shift = [], []
    for s in range(2):
        kept.append(lane_k < jnp.where(lane_q == 0, height[0][s : s + 1], height[1][s : s + 1]))
        shift.append(lane_q + jnp.where(b < 2 * c + 1 + s, 1, 0))

    def pick(a, step, s, rows):
        a = a.reshape(8, 8, 512)
        once, twice = pltpu.roll(a, step % 8, 1), pltpu.roll(a, 2 * step % 8, 1)
        a = jnp.where(shift[s][None] == 0, a, jnp.where(shift[s][None] == 1, once, twice))
        return jnp.where((kept[s] & (lane_r == rows))[None], a, 0.0).reshape(64, 512).astype(BF16)

    def section(ref, s):
        return ref[:, :, s].reshape(512, 512)

    x_load.wait()
    x = x_v[...]
    for s in range(2):
        tiles[s][0].wait()
        t = pick(dot_t(x, section(u_v, s)), -1, s, row + shift[s])
        tiles[s][1].wait()
        image = dot(t, section(v_v, s))
        for k in range(4):
            car_tmp[s, pl.ds(k, 64, stride=4), :] = image[:, 128 * k : 128 * k + 128]
        car_out[s] = car_tmp[s].reshape(HALF, CHUNK, 128).astype(BF16)

    pl.semaphore_wait(barrier, 4 + len(group))
    for copy in y_copies:
        copy.start()
    for s in range(2):
        pl.semaphore_signal(open_sem.at[s], inc=1, device_id=pairs[s][1], device_id_type=MESH)
    pl.semaphore_signal(met_sem, inc=1, device_id=below, device_id_type=MESH)

    d_load.wait()
    dg = dot_t(x, d_v[...]).reshape(8, 8, 256)
    dg = jnp.where((lane[:, :256] >> 5 == row[:, :256])[None], dg, 0.0).reshape(64, 256)
    dg = dg[:, :128] + dg[:, 128:]
    dg = dg + pltpu.roll(dg, 64, 1)
    dg = dg + pltpu.roll(dg, 32, 1)
    total = jnp.concatenate([dg] * 4, 1).reshape(8, 8, 512)
    total = jnp.where((lane >> 5 == c)[None], total, 0.0).reshape(64, 512)

    at_home = c == 2 * HALF - 1
    for s in range(2):
        pl.semaphore_wait(open_sem.at[s], 1)
        src_b, src_c = pairs[s][0]
        src_base = src_c - lax.rem(src_c, HALF)
        for i in ids + [g]:
            src, dst = car_out.at[s, i], car_in.at[s, g]
            copy = remote(src, dst, car_ssem, car_rsem, (src_b, src_base + i))
            if s == 1 and i is g:
                inside = pltpu.make_async_copy(src, dst, car_rsem)
                pl.when(at_home)(lambda: inside.start())
                pl.when(jnp.logical_not(at_home))(lambda: copy.start())
            else:
                copy.start()

    for s in range(2):
        y_copies[s].wait_recv()
        a = pick(dot_t(y_v[s], section(v_v, s)), 1, s, row)
        total = total + dot(a, section(u_v, s))
    for k in range(4):
        rs_out[pl.ds(k, 64, stride=4), :] = total[:, 128 * k : 128 * k + 128]

    def chunk(i):
        return pl.ds(pl.multiple_of(CHUNK * i, CHUNK), CHUNK)

    for i, peer in zip(ids, group):
        remote(rs_out.at[chunk(i)], rs_in.at[g], rs_ssem, rs_rsem, peer).start()
    rs_in[g] = rs_out[chunk(g), :]
    for copy in y_copies:
        copy.wait_send()

    wait_bytes(car_in, car_rsem)
    part = car_in[0, 0].astype(F32)
    for j in range(1, 2 * HALF):
        part = part + car_in[j // HALF, j % HALF].astype(F32)
    wait_bytes(rs_in.at[pl.ds(0, HALF - 1)], rs_rsem)
    for j in range(HALF):
        part = part + rs_in[j]
    zx_out[...] = part
    zx_copy = remote(zx_out, zx_in, zx_ssem, zx_rsem, across)
    pl.semaphore_wait(met_sem, 1)
    zx_copy.start()
    wait_bytes(rs_in.at[pl.ds(0, HALF - 1)], rs_ssem)
    wait_bytes(car_out.at[0], car_ssem)
    pl.when(at_home)(lambda: wait_bytes(car_out.at[1, pl.ds(0, HALF - 1)], car_ssem))
    pl.when(jnp.logical_not(at_home))(lambda: wait_bytes(car_out.at[1], car_ssem))

    zx_copy.wait_recv()
    mine = out.at[chunk(g)]
    mine[...] = part + zx_in[...]
    for peer in group:
        remote(mine, mine, ag_ssem, ag_rsem, peer).start()
    zx_copy.wait_send()
    others = out.at[pl.ds(0, CHUNK * (HALF - 1))]
    wait_bytes(others, ag_rsem)
    wait_bytes(others, ag_ssem)


def shards(probes, diag_tiles, left_factors, right_factors, ranks, present):
    hbm = pl.BlockSpec(memory_space=pltpu.HBM)
    dma = pltpu.SemaphoreType.DMA
    out = pl.pallas_call(
        kernel,
        out_shape=pltpu.VMEM((256, 128), F32),
        in_specs=[hbm] * 6,
        out_specs=pl.BlockSpec(memory_space=pltpu.VMEM),
        scratch_shapes=[
            pltpu.VMEM((64, 512), BF16),
            pltpu.VMEM((256, 512), BF16),
            pltpu.VMEM((8, 2, 2, 32, 512), BF16),
            pltpu.VMEM((8, 2, 2, 32, 512), BF16),
            pltpu.VMEM((2, 2, 8), jnp.int32),
            pltpu.VMEM((2, 2, 8), jnp.int32),
            pltpu.VMEM((2, 64, 512), BF16),
            pltpu.VMEM((2, 256, 128), F32),
            pltpu.VMEM((2, HALF, CHUNK, 128), BF16),
            pltpu.VMEM((2, HALF, CHUNK, 128), BF16),
            pltpu.VMEM((256, 128), F32),
            pltpu.VMEM((HALF, CHUNK, 128), F32),
            pltpu.VMEM((CHUNK, 128), F32),
            pltpu.VMEM((CHUNK, 128), F32),
            dma((8,)),
            dma((2,)),
            dma((2,)),
            dma,
            dma,
            dma,
            dma,
            dma,
            dma,
            dma,
            dma,
            pltpu.SemaphoreType.REGULAR,
            pltpu.SemaphoreType.REGULAR((2,)),
        ],
        compiler_params=pltpu.CompilerParams(
            collective_id=0, has_side_effects=True, vmem_limit_bytes=60 * 1024 * 1024
        ),
        cost_estimate=pl.CostEstimate(flops=300_000_000, bytes_accessed=2_500_000, transcendentals=0),
    )(
        probes.reshape(64, 512),
        diag_tiles.reshape(256, 512),
        left_factors[:, 0],
        right_factors[:, 0],
        jnp.transpose(ranks[:, 0], (1, 2, 0)),
        jnp.transpose(present[:, 0], (1, 2, 0)),
    )
    return out.reshape(8, 8, 1, 512)


def solution(mesh):
    return jax.shard_map(
        shards,
        mesh=mesh,
        in_specs=(
            P(None, None, "blk", None),
            P(None, "blk", "col", None),
            P(None, "blk", None, "col", None, None),
            P(None, "blk", None, "col", None, None),
            P(None, "blk", None, "col"),
            P(None, "blk", None, "col"),
        ),
        out_specs=P(None, None, "blk", None),
        check_vma=False,
    )
```

```python
import functools

import jax
import jax.numpy as jnp
from jax import lax
from jax.experimental import pallas as pl
from jax.experimental.pallas import tpu as pltpu
from jax.sharding import PartitionSpec as P

MESH = pl.DeviceIdType.MESH
BF16 = jnp.bfloat16
F32 = jnp.float32

NBLK = 32
HALF = 8
ZRING = 16
ZLOW = 8
CHUNK = 32


def dot(a, b):
    return lax.dot_general(a, b, (((1,), (0,)), ((), ())), preferred_element_type=F32)


def dot_t(a, b):
    return lax.dot_general(a, b, (((1,), (1,)), ((), ())), preferred_element_type=F32)


def partners(b, c, s):
    zl = lax.rem(b, ZLOW)
    zh = lax.div(c, HALF)
    g = lax.rem(c, HALF)
    z = zh * ZLOW + zl
    flip = g if s == 0 else g + 1 - 2 * lax.rem(g, 2)
    src_b = lax.rem(b + 2 * NBLK - (2 * c + 1 + s), NBLK)
    src_h = lax.rem(lax.div(z - lax.rem(src_b, ZLOW) + ZRING + 4, ZLOW), 2)
    shift = 2 * flip + 1 + s
    dst_h = lax.rem(lax.div(lax.rem(zl + shift, ZLOW) - z + ZRING + 4, ZLOW), 2)
    dst_b = lax.rem(b + shift + 16 * dst_h, NBLK)
    return (src_b, src_h * HALF + flip), (dst_b, dst_h * HALF + flip)


def quarter(b, c, up):
    zl = lax.rem(b, ZLOW)
    z = lax.rem(lax.div(c, HALF) * ZLOW + zl + up, ZRING)
    return b - zl + lax.rem(z, ZLOW), lax.div(z, ZLOW) * HALF + lax.rem(c, HALF)


def kernel(
    x_hbm, d_hbm, u_hbm, v_hbm, rank_hbm, pres_hbm, out,
    x_v, d_v, u_v, v_v, rank_v, pres_v, y_v, car_tmp, car_out, car_in, rs_out, rs_in, zx_out, zx_in,
    in_sem, y_ssem, y_rsem, car_ssem, car_rsem, rs_ssem, rs_rsem, zx_ssem, zx_rsem, ag_ssem, ag_rsem, met_sem, open_sem,
):
    b = lax.axis_index("blk")
    c = lax.axis_index("col")
    barrier = pltpu.get_barrier_semaphore()

    def greet(peers):
        for peer in peers:
            pl.semaphore_signal(barrier, inc=1, device_id=peer, device_id_type=MESH)

    def load(i, src, dst):
        copy = pltpu.make_async_copy(src, dst, in_sem.at[i])
        copy.start()
        return copy

    pairs = [partners(b, c, s) for s in range(2)]
    greet([pairs[0][0], pairs[1][0], pairs[0][1], pairs[1][1]])
    small = [load(0, rank_hbm, rank_v), load(1, pres_hbm, pres_v)]
    x_load = load(2, x_hbm, x_v)
    above, below = quarter(b, c, 4), quarter(b, c, 12)
    g = lax.rem(c, HALF)
    base = c - g
    far_first = (4, 5, 3, 2, 6, 7, 1)
    ids = [lax.rem(g + o, HALF) for o in far_first]
    group = [(b, base + i) for i in ids]
    greet([above, below] + group)
    tiles = [
        [load(3 + 2 * s, u_hbm.at[:, :, s], u_v.at[:, :, s]), load(4 + 2 * s, v_hbm.at[:, :, s], v_v.at[:, :, s])]
        for s in range(2)
    ]
    d_load = load(7, d_hbm, d_v)
    across = (b, lax.rem(c + HALF, 2 * HALF))

    def remote(src, dst, ssem, rsem, device):
        return pltpu.make_async_remote_copy(
            src_ref=src, dst_ref=dst, send_sem=ssem, recv_sem=rsem, device_id=device, device_id_type=MESH
        )

    def wait_bytes(ref, sem):
        pltpu.make_async_copy(ref, ref, sem).wait()

    y_copies = [remote(x_v, y_v.at[s], y_ssem.at[s], y_rsem.at[s], pairs[s][1]) for s in range(2)]
    for copy in small:
        copy.wait()
    lane = lax.broadcasted_iota(jnp.int32, (8, 512), 1)
    row = lax.broadcasted_iota(jnp.int32, (8, 512), 0)
    lane_r = lane >> 6
    lane_q = (lane >> 5) & 1
    lane_k = (lane & 31).astype(F32)
    spread = (row == lane_r).astype(BF16)
    height = [dot((rank_v[q] * pres_v[q]).astype(F32).astype(BF16), spread) for q in range(2)]
    kept, shift = [], []
    for s in range(2):
        kept.append(lane_k < jnp.where(lane_q == 0, height[0][s : s + 1], height[1][s : s + 1]))
        shift.append(lane_q + jnp.where(b < 2 * c + 1 + s, 1, 0))

    def pick(a, step, s, rows):
        a = a.reshape(8, 8, 512)
        once, twice = pltpu.roll(a, step % 8, 1), pltpu.roll(a, 2 * step % 8, 1)
        a = jnp.where(shift[s][None] == 0, a, jnp.where(shift[s][None] == 1, once, twice))
        return jnp.where((kept[s] & (lane_r == rows))[None], a, 0.0).reshape(64, 512).astype(BF16)

    def section(ref, s):
        return ref[:, :, s].reshape(512, 512)

    x_load.wait()
    x = x_v[...]
    for s in range(2):
        tiles[s][0].wait()
        t = pick(dot_t(x, section(u_v, s)), -1, s, row + shift[s])
        tiles[s][1].wait()
        image = dot(t, section(v_v, s))
        for k in range(4):
            car_tmp[s, pl.ds(k, 64, stride=4), :] = image[:, 128 * k : 128 * k + 128]
        car_out[s] = car_tmp[s, :256].reshape(HALF, CHUNK, 128).astype(BF16)

    d_load.wait()
    dg = dot_t(x, d_v[...]).reshape(8, 8, 256)
    dg = jnp.where((lane[:, :256] >> 5 == row[:, :256])[None], dg, 0.0).reshape(64, 256)
    dg = dg[:, :128] + dg[:, 128:]
    dg = dg + pltpu.roll(dg, 64, 1)
    dg = dg + pltpu.roll(dg, 32, 1)
    total = jnp.concatenate([dg] * 4, 1).reshape(8, 8, 512)
    total = jnp.where((lane >> 5 == c)[None], total, 0.0).reshape(64, 512)

    pl.semaphore_wait(barrier, 6 + len(group))
    for copy in y_copies:
        copy.start()
    for s in range(2):
        pl.semaphore_signal(open_sem.at[s], inc=1, device_id=pairs[s][1], device_id_type=MESH)
    pl.semaphore_signal(met_sem, inc=1, device_id=below, device_id_type=MESH)

    at_home = c == 2 * HALF - 1
    for s in range(2):
        pl.semaphore_wait(open_sem.at[s], 1)
        src_b, src_c = pairs[s][0]
        src_base = src_c - lax.rem(src_c, HALF)
        for i in ids + [g]:
            src, dst = car_out.at[s, i], car_in.at[s, g]
            copy = remote(src, dst, car_ssem, car_rsem, (src_b, src_base + i))
            if s == 1 and i is g:
                inside = pltpu.make_async_copy(src, dst, car_rsem)
                pl.when(at_home)(lambda: inside.start())
                pl.when(jnp.logical_not(at_home))(lambda: copy.start())
            else:
                copy.start()

    for s in range(2):
        y_copies[s].wait_recv()
        a = pick(dot_t(y_v[s], section(v_v, s)), 1, s, row)
        total = total + dot(a, section(u_v, s))
    for k in range(4):
        rs_out[pl.ds(k, 64, stride=4), :] = total[:, 128 * k : 128 * k + 128]

    def chunk(i):
        return pl.ds(pl.multiple_of(CHUNK * i, CHUNK), CHUNK)

    for i, peer in zip(ids, group):
        remote(rs_out.at[chunk(i)], rs_in.at[g], rs_ssem, rs_rsem, peer).start()
    rs_in[g] = rs_out[chunk(g), :]
    for copy in y_copies:
        copy.wait_send()

    wait_bytes(car_in, car_rsem)
    part = car_in[0, 0].astype(F32)
    for j in range(1, 2 * HALF):
        part = part + car_in[j // HALF, j % HALF].astype(F32)
    wait_bytes(rs_in.at[pl.ds(0, HALF - 1)], rs_rsem)
    for j in range(HALF):
        part = part + rs_in[j]
    zx_out[...] = part
    zx_copy = remote(zx_out, zx_in, zx_ssem, zx_rsem, across)
    pl.semaphore_wait(met_sem, 1)
    zx_copy.start()
    wait_bytes(rs_in.at[pl.ds(0, HALF - 1)], rs_ssem)
    wait_bytes(car_out.at[0], car_ssem)
    pl.when(at_home)(lambda: wait_bytes(car_out.at[1, pl.ds(0, HALF - 1)], car_ssem))
    pl.when(jnp.logical_not(at_home))(lambda: wait_bytes(car_out.at[1], car_ssem))

    zx_copy.wait_recv()
    mine = out.at[chunk(g)]
    mine[...] = part + zx_in[...]
    for peer in group:
        remote(mine, mine, ag_ssem, ag_rsem, peer).start()
    zx_copy.wait_send()
    others = out.at[pl.ds(0, CHUNK * (HALF - 1))]
    wait_bytes(others, ag_rsem)
    wait_bytes(others, ag_ssem)


def shards(probes, diag_tiles, left_factors, right_factors, ranks, present):
    hbm = pl.BlockSpec(memory_space=pltpu.HBM)
    dma = pltpu.SemaphoreType.DMA
    out = pl.pallas_call(
        kernel,
        out_shape=pltpu.VMEM((256, 128), F32),
        in_specs=[hbm] * 6,
        out_specs=pl.BlockSpec(memory_space=pltpu.VMEM),
        scratch_shapes=[
            pltpu.VMEM((64, 512), BF16),
            pltpu.VMEM((256, 512), BF16),
            pltpu.VMEM((8, 2, 2, 32, 512), BF16),
            pltpu.VMEM((8, 2, 2, 32, 512), BF16),
            pltpu.VMEM((2, 2, 8), jnp.int32),
            pltpu.VMEM((2, 2, 8), jnp.int32),
            pltpu.VMEM((2, 64, 512), BF16),
            pltpu.VMEM((2, 264, 128), F32),
            pltpu.VMEM((2, HALF, CHUNK, 128), BF16),
            pltpu.VMEM((2, HALF, CHUNK, 128), BF16),
            pltpu.VMEM((264, 128), F32),
            pltpu.VMEM((HALF, CHUNK, 128), F32),
            pltpu.VMEM((CHUNK, 128), F32),
            pltpu.VMEM((CHUNK, 128), F32),
            dma((8,)),
            dma((2,)),
            dma((2,)),
            dma,
            dma,
            dma,
            dma,
            dma,
            dma,
            dma,
            dma,
            pltpu.SemaphoreType.REGULAR,
            pltpu.SemaphoreType.REGULAR((2,)),
        ],
        compiler_params=pltpu.CompilerParams(
            collective_id=0, has_side_effects=True, vmem_limit_bytes=60 * 1024 * 1024
        ),
        cost_estimate=pl.CostEstimate(flops=300_000_000, bytes_accessed=2_500_000, transcendentals=0),
    )(
        probes.reshape(64, 512),
        diag_tiles.reshape(256, 512),
        left_factors[:, 0],
        right_factors[:, 0],
        jnp.transpose(ranks[:, 0], (1, 2, 0)),
        jnp.transpose(present[:, 0], (1, 2, 0)),
    )
    return out.reshape(8, 8, 1, 512)


def solution(mesh):
    return jax.shard_map(
        shards,
        mesh=mesh,
        in_specs=(
            P(None, None, "blk", None),
            P(None, "blk", "col", None),
            P(None, "blk", None, "col", None, None),
            P(None, "blk", None, "col", None, None),
            P(None, "blk", None, "col"),
            P(None, "blk", None, "col"),
        ),
        out_specs=P(None, None, "blk", None),
        check_vma=False,
    )
```
